128 devices in a mesh: dp: 8 (over y, z_hi), fsdp: 16 (over x, z_lo, core).
Axes of the slice: x: 4, y: 4, z: 4 (z_hi: 2, z_lo: 2; z = z_hi * 2 + z_lo), core: 2. Of those that a mesh axis runs over, the one named last changes fastest.
Arguments:
- tokens: bfloat16 [16384, 5120], P(('dp', 'fsdp')), may hold values from -6 to 6
- cotangent: bfloat16 [16384, 5120], P(('dp', 'fsdp')), may hold values from -6 to 6
- advantage: float32 [16384], P(('dp', 'fsdp')), may hold values from -3 to 3
- chosen: int32 [8, 16, 4], P('dp', 'fsdp'), may hold values from 0 to 127, as said below
- chosen_count: int32 [8, 16], P('dp'), may hold values from 0 to 4, as said below
- gate_weight: bfloat16 [5120, 25600], P('fsdp', 'dp'), may hold values from -0.078125 to 0.078125
- up_weight: bfloat16 [5120, 25600], P('fsdp', 'dp'), may hold values from -0.078125 to 0.078125
- down_weight: bfloat16 [25600, 5120], P('dp', 'fsdp'), may hold values from -0.0390625 to 0.0390625
Outputs:
- input_grad: bfloat16 [16384, 5120], P(('dp', 'fsdp'))
- gate_grad: bfloat16 [5120, 25600], P('fsdp', 'dp')
- up_grad: bfloat16 [5120, 25600], P('fsdp', 'dp')
- down_grad: bfloat16 [25600, 5120], P('dp', 'fsdp')
The draws below stay inside these ranges and needn't reach their ends.
Inputs may be any that keep to these rules, and one draw needn't show every extreme that they name: `chosen`: the 4 slots of one device name distinct local rows. `chosen_count`: the counts of the 16 devices that share one dp index sum to at most 32; some dp index reaches 32 and some device reaches 4 in every draw.
All inputs are finite; a program needn't handle non-finite values.
Results may differ from the reference program's by a relative error of at most 0.0058.
Values may be sent and summed in bfloat16 or wider, within the bound.
No kernel may reach another device: no remote copies, remote signals or barrier semaphores. Data moves between devices by JAX's collectives and lax.ppermute only.
A program may use at most 128 MiB of HBM per device.

```python
import jax
import jax.numpy as jnp

D = 5120
FF = 25600
ROWS_DEV = 128
CAP = 4
TOKENS = 16384
N_DP = 8
N_FSDP = 16


def draw_chosen(key, part):
    key = jax.random.fold_in(key, 11)
    subkeys = jax.random.split(key, N_DP * N_FSDP)
    picked = jax.vmap(lambda single: jax.random.permutation(single, ROWS_DEV)[:CAP])(subkeys)
    return picked.reshape(N_DP, N_FSDP, CAP).astype(jnp.int32)


def draw_chosen_count(key, part):
    key = jax.random.fold_in(key, 23)
    key_full, key_rest, key_leader, key_shuffle = jax.random.split(key, 4)
    group_total = N_FSDP * CAP // 2
    full_row = jax.random.randint(key_full, (), 0, N_DP)
    others = jax.random.randint(key_rest, (N_DP, N_FSDP), 0, 5)
    leader = jax.random.randint(key_leader, (N_DP,), 0, N_FSDP)
    column = jnp.arange(N_FSDP, dtype=jnp.int32)[None, :]
    leader_mask = column == leader[:, None]
    others = jnp.where(leader_mask, 0, jnp.minimum(others, CAP))
    before = jnp.cumsum(others, axis=1) - others
    others = jnp.minimum(others, jnp.maximum(group_total - CAP - before, 0))
    normal = jnp.where(leader_mask, CAP, others)
    shuffle = jax.random.permutation(key_shuffle, N_FSDP)
    filled = jnp.zeros((N_FSDP,), jnp.int32).at[shuffle[:N_FSDP // 2]].set(CAP)
    row_numbers = jnp.arange(N_DP, dtype=jnp.int32)[:, None]
    return jnp.where(row_numbers == full_row, filled[None, :], normal).astype(jnp.int32)


def level_of(key, dims, cuts, low, largest):
    def one(axis_at, shards_of):
        steps = jax.random.uniform(jax.random.fold_in(jax.random.fold_in(key, 6), axis_at), (shards_of,), jnp.float32, low / len(cuts), largest / len(cuts))
        return jnp.repeat(jnp.exp(steps), dims[axis_at] // shards_of).reshape((-1,) + (1,) * (len(dims) - axis_at - 1))

    factor_of = one(*cuts[0])
    for cut in cuts[1:]:
        factor_of = factor_of * one(*cut)
    return factor_of


def normal_values(rng, shape, width, most, cuts=(), kind=jnp.bfloat16):
    factor_of = level_of(rng, shape, cuts, -0.22, 0.18) if cuts else 1.0
    values = jax.random.normal(rng, shape, jnp.float32) * width * factor_of
    return jnp.minimum(jnp.maximum(values, -most), most).astype(kind)


def setup_inputs(seed: int = 0) -> dict:
    keys = jax.random.split(jax.random.key(seed), 9)
    return {
        "tokens": normal_values(keys[0], (TOKENS, D), 1.0, 6.0, ((0, 128),)),
        "cotangent": normal_values(keys[1], (TOKENS, D), 1.0, 6.0, ((0, 128),)),
        "advantage": normal_values(keys[2], (TOKENS,), 1.0, 3.0, ((0, 128),), jnp.float32),
        "chosen": draw_chosen(jax.random.fold_in(keys[8], 71), 0),
        "chosen_count": draw_chosen_count(jax.random.fold_in(keys[8], 71), 0),
        "gate_weight": normal_values(keys[5], (D, FF), D ** -0.5, 0.078125, ((0, 16), (1, 8))),
        "up_weight": normal_values(keys[6], (D, FF), D ** -0.5, 0.078125, ((0, 16), (1, 8))),
        "down_weight": normal_values(keys[7], (FF, D), FF ** -0.5, 0.0390625, ((0, 8), (1, 16))),
    }


def reference(tokens, cotangent, advantage, chosen, chosen_count, gate_weight, up_weight, down_weight):
    row_base = (jnp.arange(N_DP * N_FSDP, dtype=jnp.int32) * ROWS_DEV).reshape(N_DP, N_FSDP, 1)
    global_rows = (row_base + chosen.astype(jnp.int32)).reshape(-1)
    alive = (jnp.arange(CAP, dtype=jnp.int32)[None, None, :] < chosen_count[:, :, None]).reshape(-1)
    picked = jnp.where(alive[:, None], tokens[global_rows], jnp.zeros((), tokens.dtype))
    weighted = jnp.where(alive[:, None], cotangent[global_rows].astype(jnp.float32) * advantage[global_rows][:, None], jnp.float32(0.0)).astype(jnp.bfloat16)
    gate_pre = jnp.dot(picked, gate_weight, preferred_element_type=jnp.float32)
    up_pre = jnp.dot(picked, up_weight, preferred_element_type=jnp.float32)
    hidden_delta = jnp.dot(weighted, down_weight.T, preferred_element_type=jnp.float32)
    sigma = jax.nn.sigmoid(gate_pre)
    active = gate_pre * sigma
    hidden = (active * up_pre).astype(jnp.bfloat16)
    gate_delta = (hidden_delta * up_pre * sigma * (1.0 + gate_pre * (1.0 - sigma))).astype(jnp.bfloat16)
    up_delta = (hidden_delta * active).astype(jnp.bfloat16)
    gate_grad = jnp.dot(picked.T, gate_delta, preferred_element_type=jnp.float32).astype(jnp.bfloat16)
    up_grad = jnp.dot(picked.T, up_delta, preferred_element_type=jnp.float32).astype(jnp.bfloat16)
    down_grad = jnp.dot(hidden.T, weighted, preferred_element_type=jnp.float32).astype(jnp.bfloat16)
    selected_grad = jnp.dot(gate_delta, gate_weight.T, preferred_element_type=jnp.float32) + jnp.dot(up_delta, up_weight.T, preferred_element_type=jnp.float32)
    selected_grad = jnp.where(alive[:, None], selected_grad, jnp.float32(0.0))
    input_grad = jnp.zeros((N_DP * N_FSDP * ROWS_DEV, D), jnp.float32).at[global_rows].add(selected_grad)
    return (input_grad.astype(jnp.bfloat16), gate_grad, up_grad, down_grad)
```

```python
import jax
import jax.numpy as jnp
from jax import lax
from jax.sharding import Mesh, PartitionSpec as P

AXES = ("y", "zh", "x", "zl", "c")
SIZES = (4, 2, 4, 2, 2)
N_DP, N_FSDP, N_DEV = 8, 16, 128
CAP = 4
GROUP = 32
LIVE = N_DP * GROUP
DL = 320
FL = 3200
WIN = 1664
HI = FL - WIN
FAR = 512.0
SWAP = [(0, 1), (1, 0)]
BF, F32 = jnp.bfloat16, jnp.float32


def swiglu_backward(gate_pre, up_pre, hidden_delta):
    sigma = jax.nn.sigmoid(gate_pre)
    active = gate_pre * sigma
    hidden = (active * up_pre).astype(BF)
    gate_delta = (hidden_delta * up_pre * sigma * (1.0 + gate_pre * (1.0 - sigma))).astype(BF)
    up_delta = (hidden_delta * active).astype(BF)
    return (hidden, gate_delta, up_delta)


def dot(a, b, ca, cb):
    return lax.dot_general(a, b, (((ca,), (cb,)), ((), ())), preferred_element_type=F32)


def shards(tokens, cotangent, advantage, chosen, chosen_count, gate_weight, up_weight, down_weight):
    c = lax.axis_index("c")
    first = c == 0
    f_index = lax.axis_index(("x", "zl", "c"))
    d_index = lax.axis_index(("y", "zh"))

    def window(w, axis):
        lo = lax.slice_in_dim(w, 0, WIN, axis=axis)
        hi = lax.slice_in_dim(w, HI, FL, axis=axis)
        return jnp.where(first, lo, hi), lax.ppermute(jnp.where(first, hi, lo), "c", SWAP)

    gate_own, gate_sib = window(gate_weight, 1)
    up_own, up_sib = window(up_weight, 1)
    down_own, down_sib = window(down_weight, 0)

    counts = chosen_count[0]
    rows = chosen[0, 0]
    slots = jnp.arange(CAP, dtype=jnp.int32)
    live = slots < counts[f_index]
    before = jnp.sum(jnp.where(jnp.arange(N_FSDP) < f_index, counts, 0))
    place = jnp.where(live, d_index * GROUP + before + slots, int(FAR)).astype(BF)
    picked = jnp.where(live[:, None], tokens[rows], jnp.zeros((), BF))
    weighted = jnp.where(
        live[:, None], cotangent[rows].astype(F32) * advantage[rows][:, None], F32(0.0)
    ).astype(BF)
    message = jnp.concatenate(
        [
            picked.reshape(CAP, N_FSDP, DL),
            weighted.reshape(CAP, N_FSDP, DL),
            jnp.broadcast_to(place[:, None, None], (CAP, N_FSDP, 128)),
        ],
        axis=2,
    ).transpose(1, 0, 2)
    message = jnp.broadcast_to(message[None], (N_DP, N_FSDP, CAP, 768)).reshape(N_DEV, CAP, 768)
    got = lax.all_to_all(message, AXES, 0, 0, tiled=True).reshape(N_DEV * CAP, 768)
    pack = (jnp.arange(LIVE, dtype=jnp.int32)[:, None] == got[:, 640].astype(jnp.int32)[None, :]).astype(BF)
    own = dot(pack, got[:, :640], 1, 0).astype(BF)
    sib = lax.ppermute(own, "c", SWAP)
    x_own, y_own = own[:, :DL], own[:, DL:]
    x_sib, y_sib = sib[:, :DL], sib[:, DL:]

    gate_part = dot(x_own, gate_own, 1, 0) + dot(x_sib, gate_sib, 1, 0)
    up_part = dot(x_own, up_own, 1, 0) + dot(x_sib, up_sib, 1, 0)
    down_part = dot(y_own, down_own, 1, 1) + dot(y_sib, down_sib, 1, 1)
    parts = jnp.concatenate(
        [gate_part.astype(BF), up_part.astype(BF), down_part.astype(BF)], axis=1
    ).reshape(N_DP, GROUP, 3 * WIN)
    share = lax.all_to_all(parts, ("x", "zl"), 0, 0, tiled=True)
    share = jnp.sum(share.astype(F32), axis=0)
    hidden, gate_delta, up_delta = swiglu_backward(
        share[:, :WIN], share[:, WIN : 2 * WIN], share[:, 2 * WIN :]
    )
    values = jnp.concatenate([hidden, gate_delta, up_delta], axis=1)
    values = lax.all_to_all(
        jnp.broadcast_to(values[None], (N_DP, GROUP, 3 * WIN)), ("x", "zl"), 0, 0, tiled=True
    ).reshape(LIVE, 3 * WIN)
    other = lax.ppermute(values, "c", SWAP)
    lo = jnp.where(first, values, other)
    hi = jnp.where(first, other, values)

    def whole(k):
        return jnp.concatenate(
            [lo[:, k * WIN : (k + 1) * WIN], hi[:, k * WIN + WIN - HI : (k + 1) * WIN]], axis=1
        )

    hidden, gate_delta, up_delta = whole(0), whole(1), whole(2)

    back = dot(gate_delta, gate_weight, 1, 1) + dot(up_delta, up_weight, 1, 1)
    back = dot(pack, back.astype(BF), 0, 0).astype(BF).reshape(N_DEV, CAP, DL)
    back = lax.all_to_all(back, AXES, 0, 0, tiled=True)
    back = jnp.sum(back.reshape(N_DP, N_FSDP, CAP, DL).astype(F32), axis=0)
    back = back.transpose(1, 0, 2).reshape(CAP, N_FSDP * DL)

    gate_grad = dot(x_own, gate_delta, 0, 0).astype(BF)
    up_grad = dot(x_own, up_delta, 0, 0).astype(BF)
    down_grad = dot(hidden, y_own, 0, 0).astype(BF)

    row = jnp.arange(tokens.shape[0], dtype=jnp.int32)[:, None]
    input_grad = jnp.zeros(tokens.shape, F32)
    for s in range(CAP):
        input_grad = jnp.where((row == rows[s]) & live[s], back[s][None, :], input_grad)
    return (input_grad.astype(BF), gate_grad, up_grad, down_grad)


def solution(mesh):
    fine = Mesh(mesh.devices.reshape(SIZES), AXES)
    dp, fsdp = AXES[:2], AXES[2:]
    in_specs = (
        P(AXES, None),
        P(AXES, None),
        P(AXES),
        P(dp, fsdp, None),
        P(dp, None),
        P(fsdp, dp),
        P(fsdp, dp),
        P(dp, fsdp),
    )
    out_specs = (P(AXES, None), P(fsdp, dp), P(fsdp, dp), P(dp, fsdp))
    return jax.shard_map(shards, mesh=fine, in_specs=in_specs, out_specs=out_specs, check_vma=False)
```

```python
import jax
import jax.numpy as jnp
from jax import lax
from jax.experimental import pallas as pl
from jax.experimental.pallas import tpu as pltpu
from jax.sharding import Mesh, PartitionSpec as P

AXES = ("y", "zh", "x", "zl", "c")
SIZES = (4, 2, 4, 2, 2)
N_DP, N_FSDP, N_DEV = 8, 16, 128
CAP = 4
GROUP = 32
LIVE = N_DP * GROUP
ROWS = 128
D = 5120
DL = 320
FL = 3200
WIN = 1664
HI = FL - WIN
TILE = WIN - HI
NA, NB = 768, 896
FAR = 512
MSG = 384
SWAP = [(0, 1), (1, 0)]
BF, F32 = jnp.bfloat16, jnp.float32
SMEM = pl.BlockSpec(memory_space=pltpu.SMEM)
VMEM = pl.BlockSpec(memory_space=pltpu.VMEM)
ANY = pl.BlockSpec(memory_space=pl.ANY)
ORDER = ((0, 0), (0, 1), (1, 0), (3, 0), (2, 0), (1, 1), (3, 1), (2, 1))


def limits(mib):
    return pltpu.CompilerParams(vmem_limit_bytes=mib * 2**20)


def cost(flops, moved):
    return pl.CostEstimate(flops=flops, bytes_accessed=moved, transcendentals=0)


def dot(a, b, ca, cb):
    return lax.dot_general(a, b, (((ca,), (cb,)), ((), ())), preferred_element_type=F32)


def along(t, step):
    return lax.ppermute(t, "x", [(i, (i + step) % 4) for i in range(4)])


def up(t):
    return along(t, 1)


def down(t):
    return along(t, 3)


def ring_y(t, step):
    return lax.ppermute(t, "y", [(i, (i + step) % 4) for i in range(4)])


def across(t):
    return lax.ppermute(t, "zl", SWAP)


def sibling(t):
    return lax.ppermute(t, "c", SWAP)


def call(kernel, shapes, operands, scratch=(), mib=24, estimate=None, smem=0, out_specs=None):
    return pl.pallas_call(
        kernel,
        out_shape=[jax.ShapeDtypeStruct(s, k) for s, k in shapes],
        in_specs=[SMEM] * smem + [VMEM] * (len(operands) - smem),
        out_specs=out_specs or [VMEM] * len(shapes),
        scratch_shapes=list(scratch),
        compiler_params=limits(mib),
        cost_estimate=estimate,
    )(*operands)


def message_kernel(index, chosen_in, counts_in, advantage_in, tokens, cotangent, out,
                   chosen, counts, advantage, x_rows, y_rows, small, big):
    first = [
        pltpu.make_async_copy(chosen_in, chosen, small.at[0]),
        pltpu.make_async_copy(counts_in, counts, small.at[1]),
        pltpu.make_async_copy(advantage_in, advantage, small.at[2]),
    ]
    for copy in first:
        copy.start()
    for copy in first:
        copy.wait()
    copies = []
    for s in range(CAP):
        block = pl.ds(pl.multiple_of(chosen[0, 0, s] // 16 * 16, 16), 16)
        here = pl.ds(s * 16, 16)
        copies.append(pltpu.make_async_copy(tokens.at[block], x_rows.at[here], big.at[s]))
        copies.append(pltpu.make_async_copy(cotangent.at[block], y_rows.at[here], big.at[CAP + s]))
    for copy in copies:
        copy.start()
    f = index[0]
    count = counts[0, f]
    before = jnp.int32(0)
    for j in range(N_FSDP):
        before = before + jnp.where(j < f, counts[0, j], 0)
    row = lax.broadcasted_iota(jnp.int32, (2 * CAP, CAP * 16), 0)
    lane = lax.broadcasted_iota(jnp.int32, (2 * CAP, CAP * 16), 1)
    line = lax.broadcasted_iota(jnp.int32, (2 * CAP, 1), 0)
    wide = lax.broadcasted_iota(jnp.int32, (2 * CAP, MSG - DL), 0)
    lane_of = lax.broadcasted_iota(jnp.int32, (2 * CAP, MSG - DL), 1)
    take_x = jnp.zeros((2 * CAP, CAP * 16), F32)
    take_y = jnp.zeros((2 * CAP, CAP * 16), F32)
    scale = jnp.zeros((2 * CAP, 1), F32)
    place = jnp.where(lane_of == 0, float(FAR), 0.0)
    for s in range(CAP):
        r = chosen[0, 0, s]
        one = jnp.where(s < count, 1.0, 0.0).astype(F32)
        at = r % 16 + s * 16
        take_x = jnp.where((row == s) & (lane == at), one, take_x)
        take_y = jnp.where((row == s + CAP) & (lane == at), one, take_y)
        scale = jnp.where(line == s + CAP, advantage[r], scale)
        spot = jnp.where(s < count, before + s, FAR).astype(F32)
        place = jnp.where((wide == s) & (lane_of == 0), spot, place)
        place = jnp.where((wide == s + CAP) & (lane_of == 0), spot + GROUP, place)
        slot = (f * CAP + s + 1).astype(F32)
        place = jnp.where((wide == s) & (lane_of == 1), slot, place)
    for copy in copies:
        copy.wait()
    x = dot(take_x.astype(BF), x_rows[...], 1, 0)
    y = dot(take_y.astype(BF), y_rows[...], 1, 0) * scale
    both = (x + y).astype(BF)
    place = place.astype(BF)
    for k in range(N_FSDP):
        out[k, :, 0:DL] = both[:, k * DL : (k + 1) * DL]
        out[k, :, DL:MSG] = place


def messages(*operands):
    return pl.pallas_call(
        message_kernel,
        out_shape=jax.ShapeDtypeStruct((N_FSDP, 2 * CAP, MSG), BF),
        in_specs=[SMEM] + [ANY] * 5,
        out_specs=VMEM,
        scratch_shapes=[
            pltpu.SMEM((1, 1, CAP), jnp.int32),
            pltpu.SMEM((1, N_FSDP), jnp.int32),
            pltpu.SMEM((ROWS,), F32),
            pltpu.VMEM((CAP * 16, D), BF),
            pltpu.VMEM((CAP * 16, D), BF),
            pltpu.SemaphoreType.DMA((3,)),
            pltpu.SemaphoreType.DMA((2 * CAP,)),
        ],
        compiler_params=limits(60),
    )(*operands)


def pack_kernel(lines, out):
    spot = lax.broadcasted_iota(jnp.int32, (N_FSDP * 2 * CAP, 2 * GROUP), 1)
    place = lines[:, DL : DL + 1].astype(jnp.int32)
    out[...] = dot(jnp.where(place == spot, 1.0, 0.0).astype(BF), lines[...], 0, 0).astype(BF)


FROM_Y = (0, 3, 1, 2)


def gather_rows(index, rows, order, x, y=None):
    for k, (dx, dz) in enumerate(order):
        i = (index[1] + dx) % 4 * 2 + (index[2] + dz) % 2
        here = slice(k * GROUP, (k + 1) * GROUP)
        x[here, :] = rows[i, 0:GROUP, :]
        if y is not None:
            y[here, :] = rows[i, GROUP : 2 * GROUP, :]


RELATIVE = tuple((dx, dz) for dx in range(4) for dz in range(2))


def products(index, own, sib, weights, lo, n, scratch, store):
    xo, yo, xs, ys, tail = scratch
    gather_rows(index, own, RELATIVE, xo, yo)
    gather_rows(index, sib, RELATIVE, xs, ys)
    for k in range(3):
        a, b = (xo, xs) if k < 2 else (yo, ys)
        ends = jnp.concatenate([a[:, 256:DL], b[:, 256:DL]], axis=1)
        mine, other = weights[2 * k], weights[2 * k + 1]
        tail[0 : DL - 256, 0:n] = mine[256:DL, lo : lo + n]
        tail[DL - 256 : 128, 0:n] = other[256:DL, lo : lo + n]
        for at in range(0, n, 256):
            to = min(at + 256, n)
            total = dot(a[:, 0:256], mine[0:256, lo + at : lo + to], 1, 0)
            total += dot(b[:, 0:256], other[0:256, lo + at : lo + to], 1, 0)
            total += dot(ends, tail[:, at:to], 1, 0)
            store(slice(k * n + at, k * n + to), total)


def kernel_b(index, own, sib, w0, w1, w2, w3, w4, w5, far, near, *scratch):
    def store(cols, total):
        for dx in range(4):
            here, near_at = slice(dx * GROUP, (dx + 1) * GROUP), 2 * dx * GROUP
            near[here, cols] = total[near_at : near_at + GROUP]
            far[here, cols] = total[near_at + GROUP : near_at + 2 * GROUP].astype(BF)

    products(index, own, sib, (w0, w1, w2, w3, w4, w5), NA, NB, scratch, store)


def kernel_a(index, own, sib, w0, w1, w2, w3, w4, w5, here, right, two, left, *scratch):
    def store(cols, total):
        here[:, cols] = total[0 : 2 * GROUP]
        for k, out in enumerate((right, two, left)):
            out[:, cols] = total[(k + 1) * 2 * GROUP : (k + 2) * 2 * GROUP].astype(BF)

    products(index, own, sib, (w0, w1, w2, w3, w4, w5), 0, NA, scratch, store)


def local_products(kernel, n, shapes, *operands):
    rows = pltpu.VMEM((LIVE, MSG), BF)
    return call(
        kernel,
        [((r, 3 * n), kind) for r, kind in shapes],
        operands,
        scratch=[rows] * 4 + [pltpu.VMEM((128, n), BF)],
        smem=1,
        estimate=cost(2 * LIVE * 2 * DL * 3 * n, 10 * 2**20),
    )


def sum_b_kernel(near, far, here, right, two, left):
    here[...] = near[0:GROUP] + far[0:GROUP].astype(F32)
    for k, out in enumerate((right, two, left)):
        rows = slice((k + 1) * GROUP, (k + 2) * GROUP)
        out[...] = (near[rows] + far[rows].astype(F32)).astype(BF)


def sum_a_kernel(mine, a, b, c, here, far):
    def total(rows):
        return mine[rows] + a[rows].astype(F32) + b[rows].astype(F32) + c[rows].astype(F32)

    here[...] = total(slice(0, GROUP))
    far[...] = total(slice(GROUP, 2 * GROUP)).astype(BF)


def swiglu_backward(gate_pre, up_pre, hidden_delta):
    sigma = jax.nn.sigmoid(gate_pre)
    active = gate_pre * sigma
    hidden = active * up_pre
    gate_delta = hidden_delta * up_pre * sigma * (1.0 + gate_pre * (1.0 - sigma))
    up_delta = hidden_delta * active
    return hidden, gate_delta, up_delta


def value_kernel(index, mine_a, far_a, mine_b, right, two, left, out):
    sums_a = mine_a[...] + far_a[...].astype(F32)
    sums_b = mine_b[...] + right[...].astype(F32) + two[...].astype(F32) + left[...].astype(F32)
    of_a = swiglu_backward(*[sums_a[:, k * NA : (k + 1) * NA] for k in range(3)])
    of_b = swiglu_backward(*[sums_b[:, k * NB : (k + 1) * NB] for k in range(3)])
    unit = lax.broadcasted_iota(jnp.int32, (GROUP, NA), 1)
    keep = (unit >= TILE) | (index[3] == 0)
    for k in range(3):
        out[:, k * WIN : k * WIN + NA] = jnp.where(keep, of_a[k], 0.0).astype(BF)
        out[:, k * WIN + NA : (k + 1) * WIN] = of_b[k].astype(BF)


def split_kernel(a, b, c, *outs):
    for k, (ref, out) in enumerate(zip((a, b, c), outs)):
        out[...] = ref[:, k * WIN : (k + 1) * WIN]


def back_product(value, gate, up_w):
    return dot(value[:, WIN : 2 * WIN], gate[...], 1, 1) + dot(value[:, 2 * WIN :], up_w[...], 1, 1)


def lay_kernel(*refs):
    blocks, (gate, up_w, value, out) = refs[:-4], refs[-4:]
    for k in range(3 + (len(blocks) == 4)):
        value[k * GROUP : (k + 1) * GROUP, :] = blocks[k][...]
    if len(blocks) > 4:
        for k in range(3):
            value[3 * GROUP :, k * WIN : (k + 1) * WIN] = blocks[3 + k][...]
    out[...] = back_product(value, gate, up_w)


def back_kernel(value, gate, up_w, out):
    out[...] = back_product(value, gate, up_w)


def back_products(blocks, gate_own, gate_sib, up_own, up_sib):
    rows = 4 * GROUP
    price = cost(2 * rows * DL * 2 * WIN, 4 * 2**20)
    value, other = call(
        lay_kernel,
        [((rows, 3 * WIN), BF), ((rows, DL), F32)],
        [*blocks, gate_sib, up_sib],
        estimate=price,
    )
    mine = call(back_kernel, [((rows, DL), F32)], [value, gate_own, up_own], estimate=price)[0]
    return value, mine, sibling(other)


def unpack_kernel(index, own, mine_e, other_e, mine_l, other_l, out):
    half = DL // 2
    parts = []
    for k, (dx, dz) in enumerate(ORDER):
        i = (index[1] + dx) % 4 * 2 + (index[2] + dz) % 2
        step = sum(jnp.where(i // 2 == j, FROM_Y[j], 0) for j in range(4))
        to = (index[4] + step) % 4 * 2 + (index[5] + i % 2) % 2
        slot = own[i, 0:GROUP, MSG - 128 : MSG].astype(F32)[:, DL + 1 - (MSG - 128) : DL + 2 - (MSG - 128)]
        slot = slot.astype(jnp.int32) - 1
        line = to * (N_FSDP * 2 * CAP) + slot // CAP * (2 * CAP) + slot % CAP
        parts.append(jnp.where(slot < 0, -2 * CAP, line).astype(F32))
    line = jnp.broadcast_to(jnp.concatenate(parts, axis=0), (LIVE, 128))
    line = jnp.transpose(line)[0:1, :].astype(jnp.int32)
    back = jnp.concatenate([mine_e[...] + other_e[...], mine_l[...] + other_l[...]]).astype(BF)
    at = lax.broadcasted_iota(jnp.int32, (2 * CAP * N_DEV, LIVE), 0)
    low = jnp.where(at == line, 1.0, 0.0).astype(BF)
    high = jnp.where(at == line + CAP, 1.0, 0.0).astype(BF)
    out[...] = (dot(low, back[:, :half], 1, 0) + dot(high, back[:, half:], 1, 0)).astype(BF)


def grad_kernel(index, own_in, early_in, late_in, early_other_in, late_other_in, gate_out, up_out,
                down_out, own, mine, other, x, y, gate, up_s, down_s, reads, sems):
    top, bottom = pl.ds(0, 4 * GROUP), pl.ds(4 * GROUP, 4 * GROUP)
    loads = [
        pltpu.make_async_copy(own_in, own, reads.at[0]),
        pltpu.make_async_copy(early_in, mine.at[top], reads.at[1]),
        pltpu.make_async_copy(late_in, mine.at[bottom], reads.at[2]),
        pltpu.make_async_copy(early_other_in, other.at[top], reads.at[3]),
        pltpu.make_async_copy(late_other_in, other.at[bottom], reads.at[4]),
    ]
    for copy in loads:
        copy.start()
    c = index[3]
    loads[0].wait()
    gather_rows(index, own, ORDER, x, y)
    for copy in loads[1:]:
        copy.wait()
    starts = [pl.multiple_of(c * HI, 128), pl.multiple_of((1 - c) * HI, 128)]
    spans = [(lo, min(lo + 512, WIN)) for lo in range(0, WIN, 512)]
    copies = []
    for k, (scratch, result) in enumerate(((gate, gate_out), (up_s, up_out), (down_s, down_out))):
        part = (k + 1) % 3
        rows = (x if k < 2 else y)[:, 0:DL]

        def product(ref, lo, hi):
            return dot(rows, ref[:, part * WIN + lo : part * WIN + hi], 0, 0).astype(BF)

        for start, ref in zip(starts, (mine, other)):
            for lo, hi in spans:
                scratch[:, pl.ds(start + lo, hi - lo)] = product(ref, lo, hi)

        @pl.when(c == 0)
        def _():
            scratch[:, HI:WIN] = product(mine, HI, WIN)

        @pl.when(c == 1)
        def _():
            scratch[:, HI:WIN] = product(other, HI, WIN)

        copies.append(pltpu.make_async_copy(scratch, result, sems.at[k]))
        copies[-1].start()
    for copy in copies:
        copy.wait()


def weight_grads(*operands):
    rows, grad = pltpu.VMEM((LIVE, MSG), BF), pltpu.VMEM((DL, FL), BF)
    values = pltpu.VMEM((LIVE, 3 * WIN), BF)
    return pl.pallas_call(
        grad_kernel,
        out_shape=[jax.ShapeDtypeStruct((DL, FL), BF)] * 3,
        in_specs=[SMEM] + [ANY] * 5,
        out_specs=[ANY] * 3,
        scratch_shapes=[
            pltpu.VMEM((N_DP, 2 * GROUP, MSG), BF),
            values, values, rows, rows, grad, grad, grad,
            pltpu.SemaphoreType.DMA((5,)),
            pltpu.SemaphoreType.DMA((3,)),
        ],
        compiler_params=limits(60),
        cost_estimate=cost(2 * LIVE * DL * FL * 3, 12 * 2**20),
    )(*operands)


def shards(tokens, cotangent, advantage, chosen, chosen_count, gate_weight, up_weight, down_weight):
    c = lax.axis_index("c")
    first = c == 0
    f_index = lax.axis_index(("x", "zl", "c"))
    place = [f_index, *[lax.axis_index(a) for a in ("x", "zl", "c", "y", "zh")]]
    index = jnp.stack(place).astype(jnp.int32)
    message = messages(index, chosen, chosen_count, advantage, tokens, cotangent)
    message, gate_weight, up_weight, down_weight, chosen, chosen_count = lax.optimization_barrier(
        (message, gate_weight, up_weight, down_weight, chosen, chosen_count)
    )
    got = lax.all_to_all(message, ("x", "zl", "c"), 0, 0, tiled=True)
    packed = call(pack_kernel, [((2 * GROUP, MSG), BF)], [got.reshape(N_FSDP * 2 * CAP, MSG)])[0]
    packed = jnp.stack([packed, lax.ppermute(packed, "zh", SWAP)])
    own = jnp.concatenate([packed, ring_y(packed, 1), ring_y(packed, 3), ring_y(packed, 2)])
    sib = sibling(own)

    def window(w):
        lo, hi = w[:, :WIN], w[:, HI:]
        return jnp.where(first, lo, hi), sibling(jnp.where(first, hi, lo))

    weights = [*window(gate_weight), *window(up_weight), *window(down_weight.T)]
    rows = chosen[0, 0]
    live = jnp.arange(CAP, dtype=jnp.int32) < chosen_count[0][f_index]
    owner = ((jnp.arange(ROWS, dtype=jnp.int32)[:, None] == rows[None, :]) & live[None, :]).astype(BF)

    far, near = local_products(
        kernel_b, NB, [(4 * GROUP, BF), (4 * GROUP, F32)], index, own, sib, *weights
    )
    own_a, near = lax.optimization_barrier((own, near))
    here_a, right, two, left = local_products(
        kernel_a, NA, [(2 * GROUP, F32)] + [(2 * GROUP, BF)] * 3, index, own_a, sib, *weights
    )
    far = across(far)
    right, left, two = up(right), down(left), along(two, 2)
    shape_a, shape_b = (GROUP, 3 * NA), (GROUP, 3 * NB)
    here_b, right_b, two_b, left_b = call(
        sum_b_kernel, [(shape_b, F32)] + [(shape_b, BF)] * 3, [near, far]
    )
    here_a, far_a = call(sum_a_kernel, [(shape_a, F32), (shape_a, BF)], [here_a, right, two, left])
    far_a = across(far_a)
    right_b, left_b, two_b = up(right_b), down(left_b), along(two_b, 2)
    v00 = call(
        value_kernel,
        [((GROUP, 3 * WIN), BF)],
        [index, here_a, far_a, here_b, right_b, two_b, left_b],
        smem=1,
    )[0]

    v01, v30, v10 = across(v00), up(v00), down(v00)
    v20, v11, v31 = down(v10), across(v10), up(v01)
    part = ((GROUP, WIN), BF)
    t20, t31, t11 = call(split_kernel, [part] * 3, [v20, v31, v11])
    v21 = [across(t20), up(t31), down(t11)]
    early, mine_e, other_e = back_products([v00, v01, v10, v30], *weights[:4])
    late, mine_l, other_l = back_products([v20, v11, v31, *v21], *weights[:4])
    early_other, late_other = sibling(early), sibling(late)

    back = call(
        unpack_kernel,
        [((2 * CAP * N_DEV, DL // 2), BF)],
        [index, own, mine_e, other_e, mine_l, other_l],
        smem=1,
        estimate=cost(8 * N_DEV * 2 * LIVE * DL, 2**20),
    )[0]
    back, early_other, late_other = lax.optimization_barrier((back, early_other, late_other))
    back = lax.all_to_all(back.reshape(N_DEV, 2 * CAP, DL // 2), AXES, 0, 0, tiled=True)

    gate_grad, up_grad, down_grad = weight_grads(index, own, early, late, early_other, late_other)

    back = jnp.sum(back.reshape(N_DP, N_FSDP, 2, CAP, DL // 2).astype(F32), axis=0).astype(BF)
    back = back.transpose(2, 0, 1, 3).reshape(CAP, D)
    input_grad = dot(owner, back, 1, 0).astype(BF)
    return (input_grad, gate_grad, up_grad, down_grad.T)


def solution(mesh):
    fine = Mesh(mesh.devices.reshape(SIZES), AXES)
    dp, fsdp = AXES[:2], AXES[2:]
    in_specs = (
        P(AXES, None),
        P(AXES, None),
        P(AXES),
        P(dp, fsdp, None),
        P(dp, None),
        P(fsdp, dp),
        P(fsdp, dp),
        P(dp, fsdp),
    )
    out_specs = (P(AXES, None), P(fsdp, dp), P(fsdp, dp), P(dp, fsdp))
    return jax.shard_map(shards, mesh=fine, in_specs=in_specs, out_specs=out_specs, check_vma=False)
```

```python
import jax
import jax.numpy as jnp
from jax import lax
from jax.experimental import pallas as pl
from jax.experimental.pallas import tpu as pltpu
from jax.sharding import Mesh, PartitionSpec as P

AXES = ("y", "zh", "x", "zl", "c")
SIZES = (4, 2, 4, 2, 2)
N_DP, N_FSDP, N_DEV = 8, 16, 128
CAP = 4
GROUP = 32
LIVE = N_DP * GROUP
ROWS = 128
D = 5120
DL = 320
FL = 3200
WIN = 1664
HI = FL - WIN
TILE = WIN - HI
NA, NB = 768, 896
FAR = 512
MSG = 384
SWAP = [(0, 1), (1, 0)]
BF, F32 = jnp.bfloat16, jnp.float32
SMEM = pl.BlockSpec(memory_space=pltpu.SMEM)
VMEM = pl.BlockSpec(memory_space=pltpu.VMEM)
ANY = pl.BlockSpec(memory_space=pl.ANY)
ORDER = ((0, 0), (0, 1), (1, 0), (3, 0), (2, 0), (1, 1), (3, 1), (2, 1))


def limits(mib):
    return pltpu.CompilerParams(vmem_limit_bytes=mib * 2**20)


def cost(flops, moved):
    return pl.CostEstimate(flops=flops, bytes_accessed=moved, transcendentals=0)


def dot(a, b, ca, cb):
    return lax.dot_general(a, b, (((ca,), (cb,)), ((), ())), preferred_element_type=F32)


def along(t, step):
    return lax.ppermute(t, "x", [(i, (i + step) % 4) for i in range(4)])


def up(t):
    return along(t, 1)


def down(t):
    return along(t, 3)


def across(t):
    return lax.ppermute(t, "zl", SWAP)


def sibling(t):
    return lax.ppermute(t, "c", SWAP)


def call(kernel, shapes, operands, scratch=(), mib=16, estimate=None, smem=0, out_specs=None):
    return pl.pallas_call(
        kernel,
        out_shape=[jax.ShapeDtypeStruct(s, k) for s, k in shapes],
        in_specs=[SMEM] * smem + [VMEM] * (len(operands) - smem),
        out_specs=out_specs or [VMEM] * len(shapes),
        scratch_shapes=list(scratch),
        compiler_params=limits(mib),
        cost_estimate=estimate,
    )(*operands)


def message_kernel(chosen_in, counts_in, advantage_in, tokens, cotangent, out, owner,
                   chosen, counts, advantage, x_rows, y_rows, small, big):
    first = [
        pltpu.make_async_copy(chosen_in, chosen, small.at[0]),
        pltpu.make_async_copy(counts_in, counts, small.at[1]),
        pltpu.make_async_copy(advantage_in, advantage, small.at[2]),
    ]
    for copy in first:
        copy.start()
    for copy in first:
        copy.wait()
    copies = []
    for s in range(CAP):
        block = pl.ds(pl.multiple_of(chosen[0, 0, s] // 16 * 16, 16), 16)
        here = pl.ds(s * 16, 16)
        copies.append(pltpu.make_async_copy(tokens.at[block], x_rows.at[here], big.at[s]))
        copies.append(pltpu.make_async_copy(cotangent.at[block], y_rows.at[here], big.at[CAP + s]))
    for copy in copies:
        copy.start()
    f = lax.axis_index(("x", "zl", "c"))
    count = counts[0, f]
    before = jnp.int32(0)
    for j in range(N_FSDP):
        before = before + jnp.where(j < f, counts[0, j], 0)
    row = lax.broadcasted_iota(jnp.int32, (2 * CAP, CAP * 16), 0)
    lane = lax.broadcasted_iota(jnp.int32, (2 * CAP, CAP * 16), 1)
    line = lax.broadcasted_iota(jnp.int32, (2 * CAP, 1), 0)
    wide = lax.broadcasted_iota(jnp.int32, (2 * CAP, MSG - DL), 0)
    lane_of = lax.broadcasted_iota(jnp.int32, (2 * CAP, MSG - DL), 1)
    take_x = jnp.zeros((2 * CAP, CAP * 16), F32)
    take_y = jnp.zeros((2 * CAP, CAP * 16), F32)
    scale = jnp.zeros((2 * CAP, 1), F32)
    place = jnp.where(lane_of == 0, float(FAR), 0.0)
    for s in range(CAP):
        r = chosen[0, 0, s]
        one = jnp.where(s < count, 1.0, 0.0).astype(F32)
        at = r % 16 + s * 16
        take_x = jnp.where((row == s) & (lane == at), one, take_x)
        take_y = jnp.where((row == s + CAP) & (lane == at), one, take_y)
        scale = jnp.where(line == s + CAP, advantage[r], scale)
        spot = jnp.where(s < count, before + s, FAR).astype(F32)
        place = jnp.where((wide == s) & (lane_of == 0), spot, place)
        place = jnp.where((wide == s + CAP) & (lane_of == 0), spot + GROUP, place)
        slot = (f * CAP + s + 1).astype(F32)
        place = jnp.where((wide == s) & (lane_of == 1), slot, place)
    mark = jnp.zeros((2 * CAP, ROWS), F32)
    row = lax.broadcasted_iota(jnp.int32, (2 * CAP, ROWS), 0)
    lane = lax.broadcasted_iota(jnp.int32, (2 * CAP, ROWS), 1)
    for s in range(CAP):
        mark = jnp.where((row == s) & (lane == chosen[0, 0, s]) & (s < count), 1.0, mark)
    owner[...] = mark.astype(BF)
    for copy in copies:
        copy.wait()
    x = dot(take_x.astype(BF), x_rows[...], 1, 0)
    y = dot(take_y.astype(BF), y_rows[...], 1, 0) * scale
    both = (x + y).astype(BF)
    place = place.astype(BF)
    for k in range(N_FSDP):
        out[k, :, 0:DL] = both[:, k * DL : (k + 1) * DL]
        out[k, :, DL:MSG] = place


def messages(*operands):
    return pl.pallas_call(
        message_kernel,
        out_shape=[
            jax.ShapeDtypeStruct((N_FSDP, 2 * CAP, MSG), BF),
            jax.ShapeDtypeStruct((2 * CAP, ROWS), BF),
        ],
        in_specs=[ANY] * 5,
        out_specs=[VMEM] * 2,
        scratch_shapes=[
            pltpu.SMEM((1, 1, CAP), jnp.int32),
            pltpu.SMEM((1, N_FSDP), jnp.int32),
            pltpu.SMEM((ROWS,), F32),
            pltpu.VMEM((CAP * 16, D), BF),
            pltpu.VMEM((CAP * 16, D), BF),
            pltpu.SemaphoreType.DMA((3,)),
            pltpu.SemaphoreType.DMA((2 * CAP,)),
        ],
        compiler_params=limits(60),
    )(*operands)


def pack_kernel(lines, out):
    spot = lax.broadcasted_iota(jnp.int32, (N_FSDP * 2 * CAP, 2 * GROUP), 1)
    place = lines[:, DL : DL + 1].astype(jnp.int32)
    rows = dot(jnp.where(place == spot, 1.0, 0.0).astype(BF), lines[...], 0, 0).astype(BF)
    for i in range(N_DP):
        out[i] = rows


def gather_rows(index, rows, order, x, y=None):
    for k, (dx, dz) in enumerate(order):
        i = (index[1] + dx) % 4 * 2 + (index[2] + dz) % 2
        here = slice(k * GROUP, (k + 1) * GROUP)
        x[here, :] = rows[i, 0:GROUP, :]
        if y is not None:
            y[here, :] = rows[i, GROUP : 2 * GROUP, :]


RELATIVE = tuple((dx, dz) for dx in range(4) for dz in range(2))


def products(index, own, sib, weights, lo, n, scratch, store):
    xo, yo, xs, ys, tail = scratch
    gather_rows(index, own, RELATIVE, xo, yo)
    gather_rows(index, sib, RELATIVE, xs, ys)
    for k in range(3):
        a, b = (xo, xs) if k < 2 else (yo, ys)
        ends = jnp.concatenate([a[:, 256:DL], b[:, 256:DL]], axis=1)
        mine, other = weights[2 * k], weights[2 * k + 1]
        tail[0 : DL - 256, 0:n] = mine[256:DL, lo : lo + n]
        tail[DL - 256 : 128, 0:n] = other[256:DL, lo : lo + n]
        for at in range(0, n, 256):
            to = min(at + 256, n)
            total = dot(a[:, 0:256], mine[0:256, lo + at : lo + to], 1, 0)
            total += dot(b[:, 0:256], other[0:256, lo + at : lo + to], 1, 0)
            total += dot(ends, tail[:, at:to], 1, 0)
            store(slice(k * n + at, k * n + to), total)


def kernel_b(index, own, sib, w0, w1, w2, w3, w4, w5, far, near, *scratch):
    def store(cols, total):
        for dx in range(4):
            here, near_at = slice(dx * GROUP, (dx + 1) * GROUP), 2 * dx * GROUP
            near[here, cols] = total[near_at : near_at + GROUP]
            far[here, cols] = total[near_at + GROUP : near_at + 2 * GROUP].astype(BF)

    products(index, own, sib, (w0, w1, w2, w3, w4, w5), NA, NB, scratch, store)


def kernel_a(index, own, sib, w0, w1, w2, w3, w4, w5, here, right, two, left, *scratch):
    def store(cols, total):
        here[:, cols] = total[0 : 2 * GROUP]
        for k, out in enumerate((right, two, left)):
            out[:, cols] = total[(k + 1) * 2 * GROUP : (k + 2) * 2 * GROUP].astype(BF)

    products(index, own, sib, (w0, w1, w2, w3, w4, w5), 0, NA, scratch, store)


def local_products(kernel, n, shapes, *operands):
    rows = pltpu.VMEM((LIVE, MSG), BF)
    return call(
        kernel,
        [((r, 3 * n), kind) for r, kind in shapes],
        operands,
        scratch=[rows] * 4 + [pltpu.VMEM((128, n), BF)],
        smem=1,
        estimate=cost(2 * LIVE * 2 * DL * 3 * n, 10 * 2**20),
    )


def sum_b_kernel(near, far, here, right, two, left):
    here[...] = near[0:GROUP] + far[0:GROUP].astype(F32)
    for k, out in enumerate((right, two, left)):
        rows = slice((k + 1) * GROUP, (k + 2) * GROUP)
        out[...] = (near[rows] + far[rows].astype(F32)).astype(BF)


def sum_a_kernel(mine, a, b, c, here, far):
    def total(rows):
        return mine[rows] + a[rows].astype(F32) + b[rows].astype(F32) + c[rows].astype(F32)

    here[...] = total(slice(0, GROUP))
    far[...] = total(slice(GROUP, 2 * GROUP)).astype(BF)


def swiglu_backward(gate_pre, up_pre, hidden_delta):
    sigma = jax.nn.sigmoid(gate_pre)
    active = gate_pre * sigma
    hidden = active * up_pre
    gate_delta = hidden_delta * up_pre * sigma * (1.0 + gate_pre * (1.0 - sigma))
    up_delta = hidden_delta * active
    return hidden, gate_delta, up_delta


def value_kernel(index, mine_a, far_a, mine_b, right, two, left, out):
    sums_a = mine_a[...] + far_a[...].astype(F32)
    sums_b = mine_b[...] + right[...].astype(F32) + two[...].astype(F32) + left[...].astype(F32)
    of_a = swiglu_backward(*[sums_a[:, k * NA : (k + 1) * NA] for k in range(3)])
    of_b = swiglu_backward(*[sums_b[:, k * NB : (k + 1) * NB] for k in range(3)])
    unit = lax.broadcasted_iota(jnp.int32, (GROUP, NA), 1)
    keep = (unit >= TILE) | (index[3] == 0)
    for k in range(3):
        out[:, k * WIN : k * WIN + NA] = jnp.where(keep, of_a[k], 0.0).astype(BF)
        out[:, k * WIN + NA : (k + 1) * WIN] = of_b[k].astype(BF)


def back_kernel(*refs):
    blocks, (go, gs, uo, us, value, mine, other) = refs[:4], refs[4:]
    for k, block in enumerate(blocks):
        value[k * GROUP : (k + 1) * GROUP, :] = block[...]
    gate, up_w = value[:, WIN : 2 * WIN], value[:, 2 * WIN :]
    other[...] = dot(gate, gs[...], 1, 1) + dot(up_w, us[...], 1, 1)
    mine[...] = dot(gate, go[...], 1, 1) + dot(up_w, uo[...], 1, 1)


def back_products(blocks, weights):
    rows = 4 * GROUP
    return call(
        back_kernel,
        [((rows, 3 * WIN), BF), ((rows, DL), F32), ((rows, DL), F32)],
        [*blocks, *weights],
        estimate=cost(2 * rows * DL * 4 * WIN, 6 * 2**20),
    )


def line_kernel(index, own, out):
    parts = []
    lane = DL + 1 - (MSG - 128)
    for dx, dz in ORDER:
        i = (index[1] + dx) % 4 * 2 + (index[2] + dz) % 2
        slot = own[i, 0:GROUP, MSG - 128 : MSG].astype(F32)[:, lane : lane + 1].astype(jnp.int32) - 1
        device = slot // CAP
        line = i * (N_FSDP // 2 * 2 * CAP) + device // 2 * (2 * CAP) + slot % CAP
        core = jnp.where(slot < 0, -1, device % 2)
        parts.append(jnp.concatenate([jnp.where(core == k, line, -2 * CAP) for k in range(2)], axis=1))
    lines = jnp.concatenate(parts, axis=0).astype(F32)
    lines = jnp.concatenate([lines, jnp.zeros((LIVE, 126), F32)], axis=1)
    out[...] = jnp.transpose(lines)[0:8, :].astype(jnp.int32)


def unpack(index, core, lines, mine_e, other_e, mine_l, other_l):
    c = index[3]
    line = jnp.where(core == 0, lines[0:1, :], lines[1:2, :])
    mine = jnp.concatenate([mine_e[...], mine_l[...]])
    other = jnp.concatenate([other_e[...], other_l[...]])
    at = lax.broadcasted_iota(jnp.int32, (CAP * N_DEV, LIVE), 0)
    low = jnp.where(at == jnp.where(c == 0, line, line + CAP), 1.0, 0.0).astype(BF)
    high = jnp.where(at == jnp.where(c == 0, line + CAP, line), 1.0, 0.0).astype(BF)
    return dot(low, mine.astype(BF), 1, 0) + dot(high, other.astype(BF), 1, 0)


def unpack_send_kernel(index, lines, mine_e, other_e, mine_l, other_l, out):
    out[...] = unpack(index, 1 - index[3], lines, mine_e, other_e, mine_l, other_l).astype(BF)


def unpack_keep_kernel(index, lines, mine_e, other_e, mine_l, other_l, sent, out):
    kept = unpack(index, index[3], lines, mine_e, other_e, mine_l, other_l)
    out[...] = (kept + sent[...].astype(F32)).astype(BF)


def owner_kernel(owner, back, out):
    n = N_FSDP // 2
    for k in range(n):
        total = back[k].astype(F32)
        for i in range(1, N_DP):
            total = total + back[i * n + k].astype(F32)
        total = total.astype(BF)
        for core in range(2):
            cols = slice((2 * k + core) * DL, (2 * k + core + 1) * DL)
            rows = slice(core * CAP, (core + 1) * CAP)
            out[:, cols] = dot(owner[0:CAP, :], total[rows, :], 0, 0).astype(BF)


def grad_kernel(index, own, early_in, late_in, early_other_in, late_other_in, gate_out, up_out,
                down_out, mine, other, x, y, gate, up_s, down_s, reads, sems):
    top, bottom = pl.ds(0, 4 * GROUP), pl.ds(4 * GROUP, 4 * GROUP)
    loads = [
        pltpu.make_async_copy(early_in, mine.at[top], reads.at[0]),
        pltpu.make_async_copy(late_in, mine.at[bottom], reads.at[1]),
        pltpu.make_async_copy(early_other_in, other.at[top], reads.at[2]),
        pltpu.make_async_copy(late_other_in, other.at[bottom], reads.at[3]),
    ]
    for copy in loads:
        copy.start()
    c = index[3]
    gather_rows(index, own, ORDER, x, y)
    starts = [pl.multiple_of(c * HI, 128), pl.multiple_of((1 - c) * HI, 128)]
    spans = [(lo, min(lo + 512, WIN)) for lo in range(0, WIN, 512)]
    copies = []
    for k, (scratch, result) in enumerate(((gate, gate_out), (up_s, up_out), (down_s, down_out))):
        part = (k + 1) % 3
        rows = (x if k < 2 else y)[:, 0:DL]

        def product(ref, lo, hi):
            return dot(rows, ref[:, part * WIN + lo : part * WIN + hi], 0, 0).astype(BF)

        for start, ref, first in zip(starts, (mine, other), (0, 2)):
            if k == 0:
                loads[first].wait()
                loads[first + 1].wait()
            for lo, hi in spans:
                scratch[:, pl.ds(start + lo, hi - lo)] = product(ref, lo, hi)

        @pl.when(c == 0)
        def _():
            scratch[:, HI:WIN] = product(mine, HI, WIN)

        @pl.when(c == 1)
        def _():
            scratch[:, HI:WIN] = product(other, HI, WIN)

        copies.append(pltpu.make_async_copy(scratch, result, sems.at[k]))
        copies[-1].start()
    for copy in copies:
        copy.wait()


def weight_grads(*operands):
    rows, grad = pltpu.VMEM((LIVE, MSG), BF), pltpu.VMEM((DL, FL), BF)
    values = pltpu.VMEM((LIVE, 3 * WIN), BF)
    return pl.pallas_call(
        grad_kernel,
        out_shape=[jax.ShapeDtypeStruct((DL, FL), BF)] * 3,
        in_specs=[SMEM, VMEM] + [ANY] * 4,
        out_specs=[ANY] * 3,
        scratch_shapes=[
            values, values, rows, rows, grad, grad, grad,
            pltpu.SemaphoreType.DMA((4,)),
            pltpu.SemaphoreType.DMA((3,)),
        ],
        compiler_params=limits(60),
        cost_estimate=cost(2 * LIVE * DL * FL * 3, 12 * 2**20),
    )(*operands)


def shards(tokens, cotangent, advantage, chosen, chosen_count, gate_weight, up_weight, down_weight):
    place = [lax.axis_index(a) for a in ("c", "x", "zl", "c")]
    index = jnp.stack(place).astype(jnp.int32)
    message, owner = messages(chosen, chosen_count, advantage, tokens, cotangent)
    message, gate_weight, up_weight, down_weight = lax.optimization_barrier(
        (message, gate_weight, up_weight, down_weight)
    )
    first = lax.axis_index("c") == 0

    def window(w):
        lo, hi = w[:, :WIN], w[:, HI:]
        return jnp.where(first, lo, hi), jnp.where(first, hi, lo)

    mine, halves = [], []
    for w in (gate_weight, up_weight, down_weight.T):
        if halves:
            w, halves[-1] = lax.optimization_barrier((w, halves[-1]))
        a, b = window(w)
        mine.append(a)
        halves.append(b)
    got = lax.all_to_all(message, ("x", "zl", "c"), 0, 0, tiled=True)
    got, *halves = lax.optimization_barrier((got, *halves))
    weights = [w for pair in zip(mine, map(sibling, halves)) for w in pair]
    packed = call(pack_kernel, [((N_DP, 2 * GROUP, MSG), BF)], [got.reshape(N_FSDP * 2 * CAP, MSG)])[0]
    own = lax.all_to_all(packed, ("y", "zh"), 0, 0, tiled=True)
    sib = sibling(own)

    far, near = local_products(
        kernel_b, NB, [(4 * GROUP, BF), (4 * GROUP, F32)], index, own, sib, *weights
    )
    own_a, near = lax.optimization_barrier((own, near))
    here_a, right, two, left = local_products(
        kernel_a, NA, [(2 * GROUP, F32)] + [(2 * GROUP, BF)] * 3, index, own_a, sib, *weights
    )
    far = across(far)
    right, left, two = up(right), down(left), along(two, 2)
    shape_a, shape_b = (GROUP, 3 * NA), (GROUP, 3 * NB)
    here_b, right_b, two_b, left_b = call(
        sum_b_kernel, [(shape_b, F32)] + [(shape_b, BF)] * 3, [near, far]
    )
    here_a, far_a = call(sum_a_kernel, [(shape_a, F32), (shape_a, BF)], [here_a, right, two, left])
    far_a = across(far_a)
    right_b, left_b, two_b = up(right_b), down(left_b), along(two_b, 2)
    v00 = call(
        value_kernel,
        [((GROUP, 3 * WIN), BF)],
        [index, here_a, far_a, here_b, right_b, two_b, left_b],
        smem=1,
    )[0]

    v01, v30, v10 = lax.optimization_barrier((across(v00), up(v00), down(v00)))
    early, mine_e, other_e = back_products([v00, v01, v10, v30], weights[:4])
    lines = call(line_kernel, [((8, LIVE), jnp.int32)], [index, own], smem=1)[0]
    v20, v11, v31, early, lines = lax.optimization_barrier(
        (down(v10), across(v10), up(v01), early, lines)
    )
    v21, mine_e, other_e = lax.optimization_barrier((across(v20), mine_e, other_e))
    late, mine_l, other_l = back_products([v20, v11, v31, v21], weights[:4])
    early_other = sibling(early)

    backs = [index, lines, mine_e, other_e, mine_l, other_l]
    shape, price = (CAP * N_DEV, DL), cost(2 * CAP * N_DEV * LIVE * DL, 2**20)
    sent = call(unpack_send_kernel, [(shape, BF)], backs, smem=1, estimate=price)[0]
    sent, late = lax.optimization_barrier((sibling(sent), late))
    late_other = sibling(late)
    back = call(unpack_keep_kernel, [(shape, BF)], [*backs, sent], smem=1, estimate=price)[0]
    back, early_other = lax.optimization_barrier((back, early_other))
    back = lax.all_to_all(back.reshape(N_DEV // 2, 2 * CAP, DL), AXES[:4], 0, 0, tiled=True)

    gate_grad, up_grad, down_grad = weight_grads(index, own, early, late, early_other, late_other)

    back, down_grad = lax.optimization_barrier((back, down_grad))
    input_grad = call(owner_kernel, [((ROWS, D), BF)], [owner, back])[0]
    return (input_grad, gate_grad, up_grad, down_grad.T)


def solution(mesh):
    fine = Mesh(mesh.devices.reshape(SIZES), AXES)
    dp, fsdp = AXES[:2], AXES[2:]
    in_specs = (
        P(AXES, None),
        P(AXES, None),
        P(AXES),
        P(dp, fsdp, None),
        P(dp, None),
        P(fsdp, dp),
        P(fsdp, dp),
        P(dp, fsdp),
    )
    out_specs = (P(AXES, None), P(fsdp, dp), P(fsdp, dp), P(dp, fsdp))
    return jax.shard_map(shards, mesh=fine, in_specs=in_specs, out_specs=out_specs, check_vma=False)
```

```python
import jax
import jax.numpy as jnp
from jax import lax
from jax.experimental import pallas as pl
from jax.experimental.pallas import tpu as pltpu
from jax.sharding import Mesh, PartitionSpec as P

AXES = ("y", "zh", "x", "zl", "c")
SIZES = (4, 2, 4, 2, 2)
N_DP, N_FSDP, N_DEV = 8, 16, 128
CAP = 4
GROUP = 32
LIVE = N_DP * GROUP
ROWS = 128
D = 5120
DL = 320
FL = 3200
WIN = 1664
HI = FL - WIN
TILE = WIN - HI
NA, NB = 768, 896
FAR = 512
MSG = 384
SWAP = [(0, 1), (1, 0)]
BF, F32 = jnp.bfloat16, jnp.float32
SMEM = pl.BlockSpec(memory_space=pltpu.SMEM)
VMEM = pl.BlockSpec(memory_space=pltpu.VMEM)
ANY = pl.BlockSpec(memory_space=pl.ANY)
ORDER = ((0, 0), (0, 1), (1, 0), (3, 0), (2, 0), (1, 1), (3, 1), (2, 1))


def limits(mib):
    return pltpu.CompilerParams(vmem_limit_bytes=mib * 2**20)


def cost(flops, moved):
    return pl.CostEstimate(flops=flops, bytes_accessed=moved, transcendentals=0)


def dot(a, b, ca, cb):
    return lax.dot_general(a, b, (((ca,), (cb,)), ((), ())), preferred_element_type=F32)


def along(t, step):
    return lax.ppermute(t, "x", [(i, (i + step) % 4) for i in range(4)])


def up(t):
    return along(t, 1)


def down(t):
    return along(t, 3)


def across(t):
    return lax.ppermute(t, "zl", SWAP)


def sibling(t):
    return lax.ppermute(t, "c", SWAP)


def call(kernel, shapes, operands, scratch=(), mib=16, estimate=None, smem=0, out_specs=None):
    return pl.pallas_call(
        kernel,
        out_shape=[jax.ShapeDtypeStruct(s, k) for s, k in shapes],
        in_specs=[SMEM] * smem + [VMEM] * (len(operands) - smem),
        out_specs=out_specs or [VMEM] * len(shapes),
        scratch_shapes=list(scratch),
        compiler_params=limits(mib),
        cost_estimate=estimate,
    )(*operands)


def message_kernel(chosen_in, counts_in, advantage_in, tokens, cotangent, out, owner,
                   chosen, counts, advantage, x_rows, y_rows, small, big):
    first = [
        pltpu.make_async_copy(chosen_in, chosen, small.at[0]),
        pltpu.make_async_copy(counts_in, counts, small.at[1]),
        pltpu.make_async_copy(advantage_in, advantage, small.at[2]),
    ]
    for copy in first:
        copy.start()
    for copy in first:
        copy.wait()
    copies = []
    for s in range(CAP):
        block = pl.ds(pl.multiple_of(chosen[0, 0, s] // 16 * 16, 16), 16)
        here = pl.ds(s * 16, 16)
        copies.append(pltpu.make_async_copy(tokens.at[block], x_rows.at[here], big.at[s]))
        copies.append(pltpu.make_async_copy(cotangent.at[block], y_rows.at[here], big.at[CAP + s]))
    for copy in copies:
        copy.start()
    f = lax.axis_index(("x", "zl", "c"))
    count = counts[0, f]
    before = jnp.int32(0)
    for j in range(N_FSDP):
        before = before + jnp.where(j < f, counts[0, j], 0)
    row = lax.broadcasted_iota(jnp.int32, (2 * CAP, CAP * 16), 0)
    lane = lax.broadcasted_iota(jnp.int32, (2 * CAP, CAP * 16), 1)
    line = lax.broadcasted_iota(jnp.int32, (2 * CAP, 1), 0)
    wide = lax.broadcasted_iota(jnp.int32, (2 * CAP, MSG - DL), 0)
    lane_of = lax.broadcasted_iota(jnp.int32, (2 * CAP, MSG - DL), 1)
    take_x = jnp.zeros((2 * CAP, CAP * 16), F32)
    take_y = jnp.zeros((2 * CAP, CAP * 16), F32)
    scale = jnp.zeros((2 * CAP, 1), F32)
    d = lax.axis_index(("y", "zh"))
    place = jnp.where(lane_of < 2, float(FAR), 0.0)
    for s in range(CAP):
        r = chosen[0, 0, s]
        one = jnp.where(s < count, 1.0, 0.0).astype(F32)
        at = r % 16 + s * 16
        take_x = jnp.where((row == s) & (lane == at), one, take_x)
        take_y = jnp.where((row == s + CAP) & (lane == at), one, take_y)
        scale = jnp.where(line == s + CAP, advantage[r], scale)
        spot = jnp.where(s < count, d * GROUP + before + s, FAR).astype(F32)
        place = jnp.where((wide == s) & (lane_of == 0), spot, place)
        place = jnp.where((wide == s + CAP) & (lane_of == 1), spot, place)
        slot = (f * CAP + s + 1).astype(F32)
        place = jnp.where((wide == s) & (lane_of == 2), slot, place)
    mark = jnp.zeros((2 * CAP, ROWS), F32)
    row = lax.broadcasted_iota(jnp.int32, (2 * CAP, ROWS), 0)
    lane = lax.broadcasted_iota(jnp.int32, (2 * CAP, ROWS), 1)
    for s in range(CAP):
        mark = jnp.where((row == s) & (lane == chosen[0, 0, s]) & (s < count), 1.0, mark)
    owner[...] = mark.astype(BF)
    for copy in copies:
        copy.wait()
    x = dot(take_x.astype(BF), x_rows[...], 1, 0)
    y = dot(take_y.astype(BF), y_rows[...], 1, 0) * scale
    both = (x + y).astype(BF)
    place = place.astype(BF)
    for k in range(N_FSDP):
        part = both[:, k * DL : (k + 1) * DL]
        for i in range(N_DP):
            out[i * N_FSDP + k, :, 0:DL] = part
            out[i * N_FSDP + k, :, DL:MSG] = place


def messages(*operands):
    return pl.pallas_call(
        message_kernel,
        out_shape=[
            jax.ShapeDtypeStruct((N_DEV, 2 * CAP, MSG), BF),
            jax.ShapeDtypeStruct((2 * CAP, ROWS), BF),
        ],
        in_specs=[ANY] * 5,
        out_specs=[VMEM] * 2,
        scratch_shapes=[
            pltpu.SMEM((1, 1, CAP), jnp.int32),
            pltpu.SMEM((1, N_FSDP), jnp.int32),
            pltpu.SMEM((ROWS,), F32),
            pltpu.VMEM((CAP * 16, D), BF),
            pltpu.VMEM((CAP * 16, D), BF),
            pltpu.SemaphoreType.DMA((3,)),
            pltpu.SemaphoreType.DMA((2 * CAP,)),
        ],
        compiler_params=limits(60),
    )(*operands)


def pack_kernel(lines, out):
    places = jnp.transpose(lines[:, MSG - 128 : MSG].astype(F32)).astype(jnp.int32)
    spot = lax.broadcasted_iota(jnp.int32, (LIVE, N_DEV * 2 * CAP), 0)
    for k in range(2):
        at = DL - (MSG - 128) + k
        pack = jnp.where(places[at : at + 1, :] == spot, 1.0, 0.0).astype(BF)
        rows = dot(pack, lines[...], 1, 0).astype(BF)
        for i in range(N_DP):
            out[i, k * GROUP : (k + 1) * GROUP, :] = rows[i * GROUP : (i + 1) * GROUP]


def gather_rows(index, rows, order, x, y=None):
    for k, (dx, dz) in enumerate(order):
        i = (index[1] + dx) % 4 * 2 + (index[2] + dz) % 2
        here = slice(k * GROUP, (k + 1) * GROUP)
        x[here, :] = rows[i, 0:GROUP, :]
        if y is not None:
            y[here, :] = rows[i, GROUP : 2 * GROUP, :]


RELATIVE = tuple((dx, dz) for dx in range(4) for dz in range(2))


def products(index, own, sib, weights, lo, n, scratch, store):
    xo, yo, xs, ys, tail = scratch
    gather_rows(index, own, RELATIVE, xo, yo)
    gather_rows(index, sib, RELATIVE, xs, ys)
    for k in range(3):
        a, b = (xo, xs) if k < 2 else (yo, ys)
        ends = jnp.concatenate([a[:, 256:DL], b[:, 256:DL]], axis=1)
        mine, other = weights[2 * k], weights[2 * k + 1]
        tail[0 : DL - 256, 0:n] = mine[256:DL, lo : lo + n]
        tail[DL - 256 : 128, 0:n] = other[256:DL, lo : lo + n]
        for at in range(0, n, 256):
            to = min(at + 256, n)
            total = dot(a[:, 0:256], mine[0:256, lo + at : lo + to], 1, 0)
            total += dot(b[:, 0:256], other[0:256, lo + at : lo + to], 1, 0)
            total += dot(ends, tail[:, at:to], 1, 0)
            store(slice(k * n + at, k * n + to), total)


def kernel_b(index, own, sib, w0, w1, w2, w3, w4, w5, far0, far, near, *scratch):
    def store(cols, total):
        for dx in range(4):
            here, near_at = slice(dx * GROUP, (dx + 1) * GROUP), 2 * dx * GROUP
            near[here, cols] = total[near_at : near_at + GROUP]
            away = total[near_at + GROUP : near_at + 2 * GROUP].astype(BF)
            if dx:
                far[(dx - 1) * GROUP : dx * GROUP, cols] = away
            else:
                far0[:, cols] = away

    products(index, own, sib, (w0, w1, w2, w3, w4, w5), NA, NB, scratch, store)


def kernel_a(index, own, sib, w0, w1, w2, w3, w4, w5, here, right, two, left, *scratch):
    def store(cols, total):
        here[:, cols] = total[0 : 2 * GROUP]
        for k, out in enumerate((right, two, left)):
            out[:, cols] = total[(k + 1) * 2 * GROUP : (k + 2) * 2 * GROUP].astype(BF)

    products(index, own, sib, (w0, w1, w2, w3, w4, w5), 0, NA, scratch, store)


def local_products(kernel, n, shapes, *operands):
    rows = pltpu.VMEM((LIVE, MSG), BF)
    return call(
        kernel,
        [((r, 3 * n), kind) for r, kind in shapes],
        operands,
        scratch=[rows] * 4 + [pltpu.VMEM((128, n), BF)],
        smem=1,
        estimate=cost(2 * LIVE * 2 * DL * 3 * n, 10 * 2**20),
    )


def sum_b_kernel(near, far, right, two, left):
    for k, out in enumerate((right, two, left)):
        rows = slice((k + 1) * GROUP, (k + 2) * GROUP)
        out[...] = (near[rows] + far[k * GROUP : (k + 1) * GROUP].astype(F32)).astype(BF)


def sum_a_kernel(mine, a, b, c, here, far):
    def total(rows):
        return mine[rows] + a[rows].astype(F32) + b[rows].astype(F32) + c[rows].astype(F32)

    here[...] = total(slice(0, GROUP))
    far[...] = total(slice(GROUP, 2 * GROUP)).astype(BF)


def swiglu_backward(gate_pre, up_pre, hidden_delta):
    sigma = jax.nn.sigmoid(gate_pre)
    active = gate_pre * sigma
    hidden = active * up_pre
    gate_delta = hidden_delta * up_pre * sigma * (1.0 + gate_pre * (1.0 - sigma))
    up_delta = hidden_delta * active
    return hidden, gate_delta, up_delta


def value_kernel(index, mine_a, far_a, near, far0, right, two, left, out):
    sums_a = mine_a[...] + far_a[...].astype(F32)
    sums_b = near[0:GROUP] + far0[...].astype(F32) + right[...].astype(F32) + two[...].astype(F32) + left[...].astype(F32)
    of_a = swiglu_backward(*[sums_a[:, k * NA : (k + 1) * NA] for k in range(3)])
    of_b = swiglu_backward(*[sums_b[:, k * NB : (k + 1) * NB] for k in range(3)])
    unit = lax.broadcasted_iota(jnp.int32, (GROUP, NA), 1)
    keep = (unit >= TILE) | (index[3] == 0)
    for k in range(3):
        out[:, k * WIN : k * WIN + NA] = jnp.where(keep, of_a[k], 0.0).astype(BF)
        out[:, k * WIN + NA : (k + 1) * WIN] = of_b[k].astype(BF)


def lay_kernel(*refs):
    for k, block in enumerate(refs[:-1]):
        refs[-1][k * GROUP : (k + 1) * GROUP, :] = block[...]


def laid(blocks):
    rows = len(blocks) * GROUP
    return call(lay_kernel, [((rows, 3 * WIN), BF)], blocks, estimate=cost(0, 4 * 2**20))[0]


def back_kernel(*refs):
    value, (go, gs, uo, us, mine, other) = refs[0], refs[1:]
    gate, up_w = value[:, WIN : 2 * WIN], value[:, 2 * WIN :]
    other[...] = dot(gate, gs[...], 1, 1) + dot(up_w, us[...], 1, 1)
    mine[...] = dot(gate, go[...], 1, 1) + dot(up_w, uo[...], 1, 1)


def back_products(value, weights):
    rows = value.shape[0]
    return call(
        back_kernel,
        [((rows, DL), F32)] * 2,
        [value, *weights],
        estimate=cost(2 * rows * DL * 4 * WIN, 6 * 2**20),
    )


def line_kernel(index, own, out):
    parts = []
    lane = DL + 2 - (MSG - 128)
    for dx, dz in ORDER:
        i = (index[1] + dx) % 4 * 2 + (index[2] + dz) % 2
        slot = own[i, 0:GROUP, MSG - 128 : MSG].astype(F32)[:, lane : lane + 1].astype(jnp.int32) - 1
        device = slot // CAP
        line = i * (N_FSDP // 2 * 2 * CAP) + device // 2 * (2 * CAP) + slot % CAP
        core = jnp.where(slot < 0, -1, device % 2)
        parts.append(jnp.concatenate([jnp.where(core == k, line, -2 * CAP) for k in range(2)], axis=1))
    lines = jnp.concatenate(parts, axis=0).astype(F32)
    lines = jnp.concatenate([lines, jnp.zeros((LIVE, 126), F32)], axis=1)
    out[...] = jnp.transpose(lines)[0:8, :].astype(jnp.int32)


def unpack(index, core, lines, parts):
    c = index[3]
    line = jnp.where(core == 0, lines[0:1, :], lines[1:2, :])
    mine = jnp.concatenate([part[...] for part in parts[0::2]])
    other = jnp.concatenate([part[...] for part in parts[1::2]])
    at = lax.broadcasted_iota(jnp.int32, (CAP * N_DEV, LIVE), 0)
    low = jnp.where(at == jnp.where(c == 0, line, line + CAP), 1.0, 0.0).astype(BF)
    high = jnp.where(at == jnp.where(c == 0, line + CAP, line), 1.0, 0.0).astype(BF)
    return dot(low, mine.astype(BF), 1, 0) + dot(high, other.astype(BF), 1, 0)


def unpack_send_kernel(index, lines, *refs):
    refs[-1][...] = unpack(index, 1 - index[3], lines, refs[:-1]).astype(BF)


def unpack_keep_kernel(index, lines, *refs):
    refs[-1][...] = unpack(index, index[3], lines, refs[:-1])


def add_kernel(kept, sent, out):
    out[...] = (kept[...] + sent[...].astype(F32)).astype(BF)


def owner_kernel(owner, back, out):
    n = N_FSDP // 2
    for k in range(n):
        total = back[k].astype(F32)
        for i in range(1, N_DP):
            total = total + back[i * n + k].astype(F32)
        total = total.astype(BF)
        for core in range(2):
            cols = slice((2 * k + core) * DL, (2 * k + core + 1) * DL)
            rows = slice(core * CAP, (core + 1) * CAP)
            out[:, cols] = dot(owner[0:CAP, :], total[rows, :], 0, 0).astype(BF)


def grad_kernel(index, own, early_in, late_in, early_other_in, late_other_in, gate_out, up_out,
                down_out, mine, other, x, y, gate, up_s, down_s, reads, sems):
    top, bottom = pl.ds(0, 4 * GROUP), pl.ds(4 * GROUP, 4 * GROUP)
    loads = [
        pltpu.make_async_copy(early_in, mine.at[top], reads.at[0]),
        pltpu.make_async_copy(late_in, mine.at[bottom], reads.at[1]),
        pltpu.make_async_copy(early_other_in, other.at[top], reads.at[2]),
        pltpu.make_async_copy(late_other_in, other.at[bottom], reads.at[3]),
    ]
    for copy in loads:
        copy.start()
    c = index[3]
    gather_rows(index, own, ORDER, x, y)
    starts = [pl.multiple_of(c * HI, 128), pl.multiple_of((1 - c) * HI, 128)]
    spans = [(lo, min(lo + 512, WIN)) for lo in range(0, WIN, 512)]
    copies = []
    for k, (scratch, result) in enumerate(((gate, gate_out), (up_s, up_out), (down_s, down_out))):
        part = (k + 1) % 3
        rows = (x if k < 2 else y)[:, 0:DL]

        def product(ref, lo, hi):
            return dot(rows, ref[:, part * WIN + lo : part * WIN + hi], 0, 0).astype(BF)

        for start, ref, first in zip(starts, (mine, other), (0, 2)):
            if k == 0:
                loads[first].wait()
                loads[first + 1].wait()
            for lo, hi in spans:
                scratch[:, pl.ds(start + lo, hi - lo)] = product(ref, lo, hi)

        @pl.when(c == 0)
        def _():
            scratch[:, HI:WIN] = product(mine, HI, WIN)

        @pl.when(c == 1)
        def _():
            scratch[:, HI:WIN] = product(other, HI, WIN)

        copies.append(pltpu.make_async_copy(scratch, result, sems.at[k]))
        copies[-1].start()
    for copy in copies:
        copy.wait()


def weight_grads(*operands):
    rows, grad = pltpu.VMEM((LIVE, MSG), BF), pltpu.VMEM((DL, FL), BF)
    values = pltpu.VMEM((LIVE, 3 * WIN), BF)
    return pl.pallas_call(
        grad_kernel,
        out_shape=[jax.ShapeDtypeStruct((DL, FL), BF)] * 3,
        in_specs=[SMEM, VMEM] + [ANY] * 4,
        out_specs=[ANY] * 3,
        scratch_shapes=[
            values, values, rows, rows, grad, grad, grad,
            pltpu.SemaphoreType.DMA((4,)),
            pltpu.SemaphoreType.DMA((3,)),
        ],
        compiler_params=limits(60),
        cost_estimate=cost(2 * LIVE * DL * FL * 3, 12 * 2**20),
    )(*operands)


def shards(tokens, cotangent, advantage, chosen, chosen_count, gate_weight, up_weight, down_weight):
    place = [lax.axis_index(a) for a in ("c", "x", "zl", "c")]
    index = jnp.stack(place).astype(jnp.int32)
    message, owner = messages(chosen, chosen_count, advantage, tokens, cotangent)
    message, gate_weight, up_weight, down_weight = lax.optimization_barrier(
        (message, gate_weight, up_weight, down_weight)
    )
    first = lax.axis_index("c") == 0

    def half(w, which):
        return jnp.where(which, w[:, :WIN], w[:, HI:])

    full = [gate_weight, up_weight, down_weight.T]
    halves = []
    for w in full:
        if halves:
            w, halves[-1] = lax.optimization_barrier((w, halves[-1]))
        halves.append(half(w, ~first))
    got = lax.all_to_all(message, AXES, 0, 0, tiled=True)
    got = lax.optimization_barrier((got, *halves))[0]
    own = call(pack_kernel, [((N_DP, 2 * GROUP, MSG), BF)], [got.reshape(N_DEV * 2 * CAP, MSG)])[0]
    own, *full = lax.optimization_barrier((own, *full))
    weights = [w for f, h in zip(full, halves) for w in (half(f, first), sibling(h))]
    sib = sibling(own)

    far0, far, near = local_products(
        kernel_b, NB, [(GROUP, BF), (3 * GROUP, BF), (4 * GROUP, F32)], index, own, sib, *weights
    )
    own_a, near = lax.optimization_barrier((own, near))
    here_a, right, two, left = local_products(
        kernel_a, NA, [(2 * GROUP, F32)] + [(2 * GROUP, BF)] * 3, index, own_a, sib, *weights
    )
    far0, far = across(far0), across(far)
    right, left, two = up(right), down(left), along(two, 2)
    shape_a, shape_b = (GROUP, 3 * NA), (GROUP, 3 * NB)
    right_b, two_b, left_b = call(sum_b_kernel, [(shape_b, BF)] * 3, [near, far])
    here_a, far_a = call(sum_a_kernel, [(shape_a, F32), (shape_a, BF)], [here_a, right, two, left])
    far_a = across(far_a)
    right_b, left_b, two_b = up(right_b), down(left_b), along(two_b, 2)
    v00 = call(
        value_kernel,
        [((GROUP, 3 * WIN), BF)],
        [index, here_a, far_a, near, far0, right_b, two_b, left_b],
        smem=1,
    )[0]

    v01, v30, v10 = lax.optimization_barrier((across(v00), up(v00), down(v00)))
    early = laid([v00, v01, v10, v30])
    backs = back_products(early, weights[:4])
    lines = call(line_kernel, [((8, LIVE), jnp.int32)], [index, own], smem=1)[0]
    v20, v11, v31, early, lines = lax.optimization_barrier(
        (down(v10), across(v10), up(v01), early, lines)
    )
    v21 = across(v20)
    backs += back_products(laid([v20, v11, v31]), weights[:4])
    v21, *backs = lax.optimization_barrier((v21, *backs))
    backs += back_products(v21, weights[:4])
    early_other = sibling(early)

    backs = [index, lines, *backs]
    shape, price = (CAP * N_DEV, DL), cost(2 * CAP * N_DEV * LIVE * DL, 2**20)
    sent = call(unpack_send_kernel, [(shape, BF)], backs, smem=1, estimate=price)[0]
    v20, v21, sent = lax.optimization_barrier((v20, v21, sent))
    late = laid([v20, v11, v31, v21])
    kept = call(unpack_keep_kernel, [(shape, F32)], backs, smem=1, estimate=price)[0]
    sent, late, kept = lax.optimization_barrier((sibling(sent), late, kept))
    late_other = sibling(late)
    back = call(add_kernel, [(shape, BF)], [kept, sent])[0]
    back = lax.all_to_all(back.reshape(N_DEV // 2, 2 * CAP, DL), AXES[:4], 0, 0, tiled=True)

    gate_grad, up_grad, down_grad = weight_grads(index, own, early, late, early_other, late_other)

    back, down_grad = lax.optimization_barrier((back, down_grad))
    input_grad = call(owner_kernel, [((ROWS, D), BF)], [owner, back])[0]
    return (input_grad, gate_grad, up_grad, down_grad.T)


def solution(mesh):
    fine = Mesh(mesh.devices.reshape(SIZES), AXES)
    dp, fsdp = AXES[:2], AXES[2:]
    in_specs = (
        P(AXES, None),
        P(AXES, None),
        P(AXES),
        P(dp, fsdp, None),
        P(dp, None),
        P(fsdp, dp),
        P(fsdp, dp),
        P(dp, fsdp),
    )
    out_specs = (P(AXES, None), P(fsdp, dp), P(fsdp, dp), P(dp, fsdp))
    return jax.shard_map(shards, mesh=fine, in_specs=in_specs, out_specs=out_specs, check_vma=False)
```

```python
import jax
import jax.numpy as jnp
from jax import lax
from jax.experimental import pallas as pl
from jax.experimental.pallas import tpu as pltpu
from jax.sharding import Mesh, PartitionSpec as P

AXES = ("y", "zh", "x", "zl", "c")
SIZES = (4, 2, 4, 2, 2)
N_DP, N_FSDP, N_DEV = 8, 16, 128
CAP = 4
PART = 2560
GROUP = 32
LIVE = N_DP * GROUP
ROWS = 128
D = 5120
DL = 320
FL = 3200
WIN = 1664
HI = FL - WIN
TILE = WIN - HI
NA, NB = 768, 896
FAR = 512
MSG = 384
SWAP = [(0, 1), (1, 0)]
BF, F32 = jnp.bfloat16, jnp.float32
SMEM = pl.BlockSpec(memory_space=pltpu.SMEM)
VMEM = pl.BlockSpec(memory_space=pltpu.VMEM)
ANY = pl.BlockSpec(memory_space=pl.ANY)
ORDER = ((0, 0), (0, 1), (1, 0), (3, 0), (2, 0), (1, 1), (3, 1), (2, 1))


def limits(mib):
    return pltpu.CompilerParams(vmem_limit_bytes=mib * 2**20)


def cost(flops, moved):
    return pl.CostEstimate(flops=flops, bytes_accessed=moved, transcendentals=0)


def dot(a, b, ca, cb):
    return lax.dot_general(a, b, (((ca,), (cb,)), ((), ())), preferred_element_type=F32)


def along(t, step):
    return lax.ppermute(t, "x", [(i, (i + step) % 4) for i in range(4)])


def up(t):
    return along(t, 1)


def down(t):
    return along(t, 3)


def across(t):
    return lax.ppermute(t, "zl", SWAP)


def sibling(t):
    return lax.ppermute(t, "c", SWAP)


def call(kernel, shapes, operands, scratch=(), mib=16, estimate=None, smem=0, out_specs=None):
    return pl.pallas_call(
        kernel,
        out_shape=[jax.ShapeDtypeStruct(s, k) for s, k in shapes],
        in_specs=[SMEM] * smem + [VMEM] * (len(operands) - smem),
        out_specs=out_specs or [VMEM] * len(shapes),
        scratch_shapes=list(scratch),
        compiler_params=limits(mib),
        cost_estimate=estimate,
    )(*operands)


def message_kernel(chosen_in, counts_in, advantage_in, tokens, cotangent, out, owner,
                   chosen, counts, advantage, x_rows, y_rows, small, big):
    first = [
        pltpu.make_async_copy(chosen_in, chosen, small.at[0]),
        pltpu.make_async_copy(counts_in, counts, small.at[1]),
        pltpu.make_async_copy(advantage_in, advantage, small.at[2]),
    ]
    for copy in first:
        copy.start()
    for copy in first:
        copy.wait()
    copies = []
    for s in range(CAP):
        block = pl.ds(pl.multiple_of(chosen[0, 0, s] // 16 * 16, 16), 16)
        here = pl.ds(s * 16, 16)
        copies.append(pltpu.make_async_copy(tokens.at[block], x_rows.at[here], big.at[s]))
        copies.append(pltpu.make_async_copy(cotangent.at[block], y_rows.at[here], big.at[CAP + s]))
    for copy in copies:
        copy.start()
    f = lax.axis_index(("x", "zl", "c"))
    count = counts[0, f]
    before = jnp.int32(0)
    for j in range(N_FSDP):
        before = before + jnp.where(j < f, counts[0, j], 0)
    row = lax.broadcasted_iota(jnp.int32, (2 * CAP, CAP * 16), 0)
    lane = lax.broadcasted_iota(jnp.int32, (2 * CAP, CAP * 16), 1)
    line = lax.broadcasted_iota(jnp.int32, (2 * CAP, 1), 0)
    wide = lax.broadcasted_iota(jnp.int32, (2 * CAP, MSG - DL), 0)
    lane_of = lax.broadcasted_iota(jnp.int32, (2 * CAP, MSG - DL), 1)
    take_x = jnp.zeros((2 * CAP, CAP * 16), F32)
    take_y = jnp.zeros((2 * CAP, CAP * 16), F32)
    scale = jnp.zeros((2 * CAP, 1), F32)
    d = lax.axis_index(("y", "zh"))
    place = jnp.where(lane_of < 2, float(FAR), 0.0)
    for s in range(CAP):
        r = chosen[0, 0, s]
        one = jnp.where(s < count, 1.0, 0.0).astype(F32)
        at = r % 16 + s * 16
        take_x = jnp.where((row == s) & (lane == at), one, take_x)
        take_y = jnp.where((row == s + CAP) & (lane == at), one, take_y)
        scale = jnp.where(line == s + CAP, advantage[r], scale)
        spot = jnp.where(s < count, d * GROUP + before + s, FAR).astype(F32)
        place = jnp.where((wide == s) & (lane_of == 0), spot, place)
        place = jnp.where((wide == s + CAP) & (lane_of == 1), spot, place)
        slot = (f * CAP + s + 1).astype(F32)
        place = jnp.where((wide == s) & (lane_of == 2), slot, place)
    mark = jnp.zeros((2 * CAP, ROWS), F32)
    row = lax.broadcasted_iota(jnp.int32, (2 * CAP, ROWS), 0)
    lane = lax.broadcasted_iota(jnp.int32, (2 * CAP, ROWS), 1)
    for s in range(CAP):
        mark = jnp.where((row == s) & (lane == chosen[0, 0, s]) & (s < count), 1.0, mark)
    owner[...] = mark.astype(BF)
    for copy in copies:
        copy.wait()
    x = dot(take_x.astype(BF), x_rows[...], 1, 0)
    y = dot(take_y.astype(BF), y_rows[...], 1, 0) * scale
    both = (x + y).astype(BF)
    place = place.astype(BF)
    for k in range(N_FSDP):
        part = both[:, k * DL : (k + 1) * DL]
        for i in range(N_DP):
            out[i * N_FSDP + k, :, 0:DL] = part
            out[i * N_FSDP + k, :, DL:MSG] = place


def messages(*operands):
    return pl.pallas_call(
        message_kernel,
        out_shape=[
            jax.ShapeDtypeStruct((N_DEV, 2 * CAP, MSG), BF),
            jax.ShapeDtypeStruct((2 * CAP, ROWS), BF),
        ],
        in_specs=[ANY] * 5,
        out_specs=[VMEM] * 2,
        scratch_shapes=[
            pltpu.SMEM((1, 1, CAP), jnp.int32),
            pltpu.SMEM((1, N_FSDP), jnp.int32),
            pltpu.SMEM((ROWS,), F32),
            pltpu.VMEM((CAP * 16, D), BF),
            pltpu.VMEM((CAP * 16, D), BF),
            pltpu.SemaphoreType.DMA((3,)),
            pltpu.SemaphoreType.DMA((2 * CAP,)),
        ],
        compiler_params=limits(60),
    )(*operands)


def pack_kernel(lines, out):
    places = jnp.transpose(lines[:, MSG - 128 : MSG].astype(F32)).astype(jnp.int32)
    spot = lax.broadcasted_iota(jnp.int32, (LIVE, N_DEV * 2 * CAP), 0)
    for k in range(2):
        at = DL - (MSG - 128) + k
        pack = jnp.where(places[at : at + 1, :] == spot, 1.0, 0.0).astype(BF)
        rows = dot(pack, lines[...], 1, 0).astype(BF)
        for i in range(N_DP):
            out[i, k * GROUP : (k + 1) * GROUP, :] = rows[i * GROUP : (i + 1) * GROUP]


def gather_rows(index, rows, order, x, y=None):
    for k, (dx, dz) in enumerate(order):
        i = (index[1] + dx) % 4 * 2 + (index[2] + dz) % 2
        here = slice(k * GROUP, (k + 1) * GROUP)
        x[here, :] = rows[i, 0:GROUP, :]
        if y is not None:
            y[here, :] = rows[i, GROUP : 2 * GROUP, :]


RELATIVE = tuple((dx, dz) for dx in range(4) for dz in range(2))


def products(index, own, sib, weights, lo, n, scratch, store):
    xo, yo, xs, ys, tail = scratch
    gather_rows(index, own, RELATIVE, xo, yo)
    gather_rows(index, sib, RELATIVE, xs, ys)
    for k in range(3):
        a, b = (xo, xs) if k < 2 else (yo, ys)
        ends = jnp.concatenate([a[:, 256:DL], b[:, 256:DL]], axis=1)
        mine, other = weights[2 * k], weights[2 * k + 1]
        tail[0 : DL - 256, 0:n] = mine[256:DL, lo : lo + n]
        tail[DL - 256 : 128, 0:n] = other[256:DL, lo : lo + n]
        for at in range(0, n, 256):
            to = min(at + 256, n)
            total = dot(a[:, 0:256], mine[0:256, lo + at : lo + to], 1, 0)
            total += dot(b[:, 0:256], other[0:256, lo + at : lo + to], 1, 0)
            total += dot(ends, tail[:, at:to], 1, 0)
            store(slice(k * n + at, k * n + to), total)


def kernel_b(index, own, sib, w0, w1, w2, w3, w4, w5, far0, far, near, *scratch):
    def store(cols, total):
        for dx in range(4):
            here, near_at = slice(dx * GROUP, (dx + 1) * GROUP), 2 * dx * GROUP
            near[here, cols] = total[near_at : near_at + GROUP]
            away = total[near_at + GROUP : near_at + 2 * GROUP].astype(BF)
            if dx:
                far[(dx - 1) * GROUP : dx * GROUP, cols] = away
            else:
                far0[:, cols] = away

    products(index, own, sib, (w0, w1, w2, w3, w4, w5), NA, NB, scratch, store)


def kernel_a(index, own, sib, w0, w1, w2, w3, w4, w5, here, right, two, left, *scratch):
    def store(cols, total):
        here[:, cols] = total[0 : 2 * GROUP]
        for k, out in enumerate((right, two, left)):
            out[:, cols] = total[(k + 1) * 2 * GROUP : (k + 2) * 2 * GROUP].astype(BF)

    products(index, own, sib, (w0, w1, w2, w3, w4, w5), 0, NA, scratch, store)


def local_products(kernel, n, shapes, *operands):
    rows = pltpu.VMEM((LIVE, MSG), BF)
    return call(
        kernel,
        [((r, 3 * n), kind) for r, kind in shapes],
        operands,
        scratch=[rows] * 4 + [pltpu.VMEM((128, n), BF)],
        smem=1,
        estimate=cost(2 * LIVE * 2 * DL * 3 * n, 10 * 2**20),
    )


def sum_b_kernel(near, far, right, two, left):
    for k, out in enumerate((right, two, left)):
        rows = slice((k + 1) * GROUP, (k + 2) * GROUP)
        out[...] = (near[rows] + far[k * GROUP : (k + 1) * GROUP].astype(F32)).astype(BF)


def sum_a_kernel(mine, a, b, c, here, far):
    def total(rows):
        return mine[rows] + a[rows].astype(F32) + b[rows].astype(F32) + c[rows].astype(F32)

    here[...] = total(slice(0, GROUP))
    far[...] = total(slice(GROUP, 2 * GROUP)).astype(BF)


def swiglu_backward(gate_pre, up_pre, hidden_delta):
    sigma = jax.nn.sigmoid(gate_pre)
    active = gate_pre * sigma
    hidden = active * up_pre
    gate_delta = hidden_delta * up_pre * sigma * (1.0 + gate_pre * (1.0 - sigma))
    up_delta = hidden_delta * active
    return hidden, gate_delta, up_delta


def value_kernel(index, mine_a, far_a, near, far0, right, two, left, out, piece, rest):
    sums_a = mine_a[...] + far_a[...].astype(F32)
    sums_b = near[0:GROUP] + far0[...].astype(F32) + right[...].astype(F32) + two[...].astype(F32) + left[...].astype(F32)
    of_a = swiglu_backward(*[sums_a[:, k * NA : (k + 1) * NA] for k in range(3)])
    of_b = swiglu_backward(*[sums_b[:, k * NB : (k + 1) * NB] for k in range(3)])
    unit = lax.broadcasted_iota(jnp.int32, (GROUP, NA), 1)
    keep = (unit >= TILE) | (index[3] == 0)
    for k in range(3):
        out[:, k * WIN : k * WIN + NA] = jnp.where(keep, of_a[k], 0.0).astype(BF)
        out[:, k * WIN + NA : (k + 1) * WIN] = of_b[k].astype(BF)
    piece[...] = out[:, :PART]
    rest[...] = out[:, PART:]


def lay_kernel(*refs):
    row = col = 0
    for block in refs[:-1]:
        width = block.shape[1]
        refs[-1][row * GROUP : (row + 1) * GROUP, col : col + width] = block[...]
        row, col = (row + 1, 0) if col + width == 3 * WIN else (row, width)


def laid(blocks):
    rows = sum(block.shape[1] for block in blocks) // (3 * WIN) * GROUP
    return call(lay_kernel, [((rows, 3 * WIN), BF)], blocks, estimate=cost(0, 4 * 2**20))[0]


def back_kernel(*refs):
    value, (go, gs, uo, us, mine, other) = refs[0], refs[1:]
    gate, up_w = value[:, WIN : 2 * WIN], value[:, 2 * WIN :]
    other[...] = dot(gate, gs[...], 1, 1) + dot(up_w, us[...], 1, 1)
    mine[...] = dot(gate, go[...], 1, 1) + dot(up_w, uo[...], 1, 1)


def back_products(value, weights):
    rows = value.shape[0]
    return call(
        back_kernel,
        [((rows, DL), F32)] * 2,
        [value, *weights],
        estimate=cost(2 * rows * DL * 4 * WIN, 6 * 2**20),
    )


def line_kernel(index, own, out):
    parts = []
    lane = DL + 2 - (MSG - 128)
    for dx, dz in ORDER:
        i = (index[1] + dx) % 4 * 2 + (index[2] + dz) % 2
        slot = own[i, 0:GROUP, MSG - 128 : MSG].astype(F32)[:, lane : lane + 1].astype(jnp.int32) - 1
        device = slot // CAP
        line = i * (N_FSDP // 2 * 2 * CAP) + device // 2 * (2 * CAP) + slot % CAP
        core = jnp.where(slot < 0, -1, device % 2)
        parts.append(jnp.concatenate([jnp.where(core == k, line, -2 * CAP) for k in range(2)], axis=1))
    lines = jnp.concatenate(parts, axis=0).astype(F32)
    lines = jnp.concatenate([lines, jnp.zeros((LIVE, 126), F32)], axis=1)
    out[...] = jnp.transpose(lines)[0:8, :].astype(jnp.int32)


def unpack(index, core, lines, parts, start=0):
    c = index[3]
    line = jnp.where(core == 0, lines[0:1, :], lines[1:2, :])
    mine = jnp.concatenate([part[...] for part in parts[0::2]])
    other = jnp.concatenate([part[...] for part in parts[1::2]])
    rows = mine.shape[0]
    line = line[:, start : start + rows]
    at = lax.broadcasted_iota(jnp.int32, (CAP * N_DEV, rows), 0)
    low = jnp.where(at == jnp.where(c == 0, line, line + CAP), 1.0, 0.0).astype(BF)
    high = jnp.where(at == jnp.where(c == 0, line + CAP, line), 1.0, 0.0).astype(BF)
    return dot(low, mine.astype(BF), 1, 0) + dot(high, other.astype(BF), 1, 0)


def unpack_early_kernel(index, lines, *refs):
    refs[-1][...] = unpack(index, 1 - index[3], lines, refs[:-1])


def unpack_last_kernel(index, lines, sent, value, go, gs, uo, us, mine, other, out):
    back_kernel(value, go, gs, uo, us, mine, other)
    last = unpack(index, 1 - index[3], lines, (mine, other), LIVE - GROUP)
    out[...] = (sent[...] + last).astype(BF)


def unpack_keep_kernel(index, lines, *refs):
    refs[-1][...] = unpack(index, index[3], lines, refs[:-1])


def add_kernel(kept, sent, out):
    out[...] = (kept[...] + sent[...].astype(F32)).astype(BF)


def owner_kernel(owner, back, out):
    n = N_FSDP // 2
    for k in range(n):
        total = back[k].astype(F32)
        for i in range(1, N_DP):
            total = total + back[i * n + k].astype(F32)
        total = total.astype(BF)
        for core in range(2):
            cols = slice((2 * k + core) * DL, (2 * k + core + 1) * DL)
            rows = slice(core * CAP, (core + 1) * CAP)
            out[:, cols] = dot(owner[0:CAP, :], total[rows, :], 0, 0).astype(BF)


def grad_kernel(index, own, early_in, late_in, early_other_in, late_other_in, gate_out, up_out,
                down_out, mine, other, x, y, gate, up_s, down_s, reads, sems):
    top, bottom = pl.ds(0, 4 * GROUP), pl.ds(4 * GROUP, 4 * GROUP)
    loads = [
        pltpu.make_async_copy(early_in, mine.at[top], reads.at[0]),
        pltpu.make_async_copy(late_in, mine.at[bottom], reads.at[1]),
        pltpu.make_async_copy(early_other_in, other.at[top], reads.at[2]),
        pltpu.make_async_copy(late_other_in, other.at[bottom], reads.at[3]),
    ]
    for copy in loads:
        copy.start()
    c = index[3]
    gather_rows(index, own, ORDER, x, y)
    starts = [pl.multiple_of(c * HI, 128), pl.multiple_of((1 - c) * HI, 128)]
    spans = [(lo, min(lo + 512, WIN)) for lo in range(0, WIN, 512)]
    copies = []
    for k, (scratch, result) in enumerate(((gate, gate_out), (up_s, up_out), (down_s, down_out))):
        part = (k + 1) % 3
        rows = (x if k < 2 else y)[:, 0:DL]

        def product(ref, lo, hi):
            return dot(rows, ref[:, part * WIN + lo : part * WIN + hi], 0, 0).astype(BF)

        for start, ref, first in zip(starts, (mine, other), (0, 2)):
            if k == 0:
                loads[first].wait()
                loads[first + 1].wait()
            for lo, hi in spans:
                scratch[:, pl.ds(start + lo, hi - lo)] = product(ref, lo, hi)

        @pl.when(c == 0)
        def _():
            scratch[:, HI:WIN] = product(mine, HI, WIN)

        @pl.when(c == 1)
        def _():
            scratch[:, HI:WIN] = product(other, HI, WIN)

        copies.append(pltpu.make_async_copy(scratch, result, sems.at[k]))
        copies[-1].start()
    for copy in copies:
        copy.wait()


def weight_grads(*operands):
    rows, grad = pltpu.VMEM((LIVE, MSG), BF), pltpu.VMEM((DL, FL), BF)
    values = pltpu.VMEM((LIVE, 3 * WIN), BF)
    return pl.pallas_call(
        grad_kernel,
        out_shape=[jax.ShapeDtypeStruct((DL, FL), BF)] * 3,
        in_specs=[SMEM, VMEM] + [ANY] * 4,
        out_specs=[ANY] * 3,
        scratch_shapes=[
            values, values, rows, rows, grad, grad, grad,
            pltpu.SemaphoreType.DMA((4,)),
            pltpu.SemaphoreType.DMA((3,)),
        ],
        compiler_params=limits(60),
        cost_estimate=cost(2 * LIVE * DL * FL * 3, 12 * 2**20),
    )(*operands)


def shards(tokens, cotangent, advantage, chosen, chosen_count, gate_weight, up_weight, down_weight):
    place = [lax.axis_index(a) for a in ("c", "x", "zl", "c")]
    index = jnp.stack(place).astype(jnp.int32)
    message, owner = messages(chosen, chosen_count, advantage, tokens, cotangent)
    message, gate_weight, up_weight, down_weight = lax.optimization_barrier(
        (message, gate_weight, up_weight, down_weight)
    )
    first = lax.axis_index("c") == 0

    def half(w, which):
        return jnp.where(which, w[:, :WIN], w[:, HI:])

    full = [gate_weight, up_weight, down_weight.T]
    halves = []
    for w in full:
        if halves:
            w, halves[-1] = lax.optimization_barrier((w, halves[-1]))
        halves.append(half(w, ~first))
    got = lax.all_to_all(message, AXES, 0, 0, tiled=True)
    got = lax.optimization_barrier((got, *halves))[0]
    own = call(pack_kernel, [((N_DP, 2 * GROUP, MSG), BF)], [got.reshape(N_DEV * 2 * CAP, MSG)])[0]
    own, *full = lax.optimization_barrier((own, *full))
    weights = [w for f, h in zip(full, halves) for w in (half(f, first), sibling(h))]
    sib = sibling(own)

    far0, far, near = local_products(
        kernel_b, NB, [(GROUP, BF), (3 * GROUP, BF), (4 * GROUP, F32)], index, own, sib, *weights
    )
    own_a, near = lax.optimization_barrier((own, near))
    here_a, right, two, left = local_products(
        kernel_a, NA, [(2 * GROUP, F32)] + [(2 * GROUP, BF)] * 3, index, own_a, sib, *weights
    )
    far0, far = across(far0), across(far)
    right, left, two = up(right), down(left), along(two, 2)
    shape_a, shape_b = (GROUP, 3 * NA), (GROUP, 3 * NB)
    right_b, two_b, left_b = call(sum_b_kernel, [(shape_b, BF)] * 3, [near, far])
    here_a, far_a = call(sum_a_kernel, [(shape_a, F32), (shape_a, BF)], [here_a, right, two, left])
    far_a = across(far_a)
    right_b, left_b, two_b = up(right_b), down(left_b), along(two_b, 2)
    v00, *p00 = call(
        value_kernel,
        [((GROUP, 3 * WIN), BF), ((GROUP, PART), BF), ((GROUP, 3 * WIN - PART), BF)],
        [index, here_a, far_a, near, far0, right_b, two_b, left_b],
        smem=1,
    )

    v10 = [down(p) for p in p00]
    v01, v30 = across(v00), up(v00)
    v10[0], v30 = lax.optimization_barrier((v10[0], v30))
    v10[1], v01 = lax.optimization_barrier((v10[1], v01))
    v20 = [down(p) for p in v10]
    v11 = [across(p) for p in v10]
    v31 = up(v01)
    early = laid([v00, v01, *v10, v30])
    backs = back_products(early, weights[:4])
    lines = call(line_kernel, [((8, LIVE), jnp.int32)], [index, own], smem=1)[0]
    v20[1], v31, early, lines = lax.optimization_barrier((v20[1], v31, early, lines))
    v21 = [across(p) for p in v20]
    backs += back_products(laid([*v20, *v11, v31]), weights[:4])
    shape, price = (CAP * N_DEV, DL), cost(2 * CAP * N_DEV * LIVE * DL, 2**20)
    sent = call(unpack_early_kernel, [(shape, F32)], [index, lines, *backs], smem=1, estimate=price)[0]
    v21[0], v21[1], sent, *backs = lax.optimization_barrier((*v21, sent, *backs))
    last = laid(v21)
    mine, other, sent = call(
        unpack_last_kernel,
        [((GROUP, DL), F32)] * 2 + [(shape, BF)],
        [index, lines, sent, last, *weights[:4]],
        smem=1,
        estimate=price,
    )
    backs += [mine, other]
    early_other = sibling(early)

    backs = [index, lines, *backs]
    last, sent = lax.optimization_barrier((last, sent))
    late = laid([*v20, *v11, v31, last])
    kept = call(unpack_keep_kernel, [(shape, F32)], backs, smem=1, estimate=price)[0]
    sent, late, kept = lax.optimization_barrier((sibling(sent), late, kept))
    late_other = sibling(late)
    back = call(add_kernel, [(shape, BF)], [kept, sent])[0]
    back = lax.all_to_all(back.reshape(N_DEV // 2, 2 * CAP, DL), AXES[:4], 0, 0, tiled=True)

    gate_grad, up_grad, down_grad = weight_grads(index, own, early, late, early_other, late_other)

    back, down_grad = lax.optimization_barrier((back, down_grad))
    input_grad = call(owner_kernel, [((ROWS, D), BF)], [owner, back])[0]
    return (input_grad, gate_grad, up_grad, down_grad.T)


def solution(mesh):
    fine = Mesh(mesh.devices.reshape(SIZES), AXES)
    dp, fsdp = AXES[:2], AXES[2:]
    in_specs = (
        P(AXES, None),
        P(AXES, None),
        P(AXES),
        P(dp, fsdp, None),
        P(dp, None),
        P(fsdp, dp),
        P(fsdp, dp),
        P(dp, fsdp),
    )
    out_specs = (P(AXES, None), P(fsdp, dp), P(fsdp, dp), P(dp, fsdp))
    return jax.shard_map(shards, mesh=fine, in_specs=in_specs, out_specs=out_specs, check_vma=False)
```

```python
import jax
import jax.numpy as jnp
from jax import lax
from jax.experimental import pallas as pl
from jax.experimental.pallas import tpu as pltpu
from jax.sharding import Mesh, PartitionSpec as P

AXES = ("y", "zh", "x", "zl", "c")
SIZES = (4, 2, 4, 2, 2)
N_DP, N_FSDP, N_DEV = 8, 16, 128
CAP = 4
PART = 2560
GROUP = 32
LIVE = N_DP * GROUP
ROWS = 128
D = 5120
DL = 320
FL = 3200
WIN = 1664
HI = FL - WIN
TILE = WIN - HI
NA, NB = 768, 896
FAR = 512
MSG = 384
SWAP = [(0, 1), (1, 0)]
BF, F32 = jnp.bfloat16, jnp.float32
SMEM = pl.BlockSpec(memory_space=pltpu.SMEM)
VMEM = pl.BlockSpec(memory_space=pltpu.VMEM)
ANY = pl.BlockSpec(memory_space=pl.ANY)
ORDER = ((0, 0), (0, 1), (1, 0), (3, 0), (2, 0), (1, 1), (3, 1), (2, 1))


def limits(mib):
    return pltpu.CompilerParams(vmem_limit_bytes=mib * 2**20)


def cost(flops, moved):
    return pl.CostEstimate(flops=flops, bytes_accessed=moved, transcendentals=0)


def dot(a, b, ca, cb):
    return lax.dot_general(a, b, (((ca,), (cb,)), ((), ())), preferred_element_type=F32)


def along(t, step):
    return lax.ppermute(t, "x", [(i, (i + step) % 4) for i in range(4)])


def up(t):
    return along(t, 1)


def down(t):
    return along(t, 3)


def across(t):
    return lax.ppermute(t, "zl", SWAP)


def sibling(t):
    return lax.ppermute(t, "c", SWAP)


def call(kernel, shapes, operands, scratch=(), mib=16, estimate=None, smem=0, out_specs=None):
    return pl.pallas_call(
        kernel,
        out_shape=[jax.ShapeDtypeStruct(s, k) for s, k in shapes],
        in_specs=[SMEM] * smem + [VMEM] * (len(operands) - smem),
        out_specs=out_specs or [VMEM] * len(shapes),
        scratch_shapes=list(scratch),
        compiler_params=limits(mib),
        cost_estimate=estimate,
    )(*operands)


def message_kernel(chosen_in, counts_in, advantage_in, tokens, cotangent, out, owner,
                   chosen, counts, advantage, x_rows, y_rows, small, big):
    first = [
        pltpu.make_async_copy(chosen_in, chosen, small.at[0]),
        pltpu.make_async_copy(counts_in, counts, small.at[1]),
        pltpu.make_async_copy(advantage_in, advantage, small.at[2]),
    ]
    for copy in first:
        copy.start()
    for copy in first:
        copy.wait()
    copies = []
    for s in range(CAP):
        block = pl.ds(pl.multiple_of(chosen[0, 0, s] // 16 * 16, 16), 16)
        here = pl.ds(s * 16, 16)
        copies.append(pltpu.make_async_copy(tokens.at[block], x_rows.at[here], big.at[s]))
        copies.append(pltpu.make_async_copy(cotangent.at[block], y_rows.at[here], big.at[CAP + s]))
    for copy in copies:
        copy.start()
    f = lax.axis_index(("x", "zl", "c"))
    count = counts[0, f]
    before = jnp.int32(0)
    for j in range(N_FSDP):
        before = before + jnp.where(j < f, counts[0, j], 0)
    row = lax.broadcasted_iota(jnp.int32, (2 * CAP, CAP * 16), 0)
    lane = lax.broadcasted_iota(jnp.int32, (2 * CAP, CAP * 16), 1)
    line = lax.broadcasted_iota(jnp.int32, (2 * CAP, 1), 0)
    wide = lax.broadcasted_iota(jnp.int32, (2 * CAP, MSG - DL), 0)
    lane_of = lax.broadcasted_iota(jnp.int32, (2 * CAP, MSG - DL), 1)
    take_x = jnp.zeros((2 * CAP, CAP * 16), F32)
    take_y = jnp.zeros((2 * CAP, CAP * 16), F32)
    scale = jnp.zeros((2 * CAP, 1), F32)
    d = lax.axis_index(("y", "zh"))
    place = jnp.where(lane_of < 2, float(FAR), 0.0)
    for s in range(CAP):
        r = chosen[0, 0, s]
        one = jnp.where(s < count, 1.0, 0.0).astype(F32)
        at = r % 16 + s * 16
        take_x = jnp.where((row == s) & (lane == at), one, take_x)
        take_y = jnp.where((row == s + CAP) & (lane == at), one, take_y)
        scale = jnp.where(line == s + CAP, advantage[r], scale)
        spot = jnp.where(s < count, d * GROUP + before + s, FAR).astype(F32)
        place = jnp.where((wide == s) & (lane_of == 0), spot, place)
        place = jnp.where((wide == s + CAP) & (lane_of == 1), spot, place)
        slot = (f * CAP + s + 1).astype(F32)
        place = jnp.where((wide == s) & (lane_of == 2), slot, place)
    mark = jnp.zeros((2 * CAP, ROWS), F32)
    row = lax.broadcasted_iota(jnp.int32, (2 * CAP, ROWS), 0)
    lane = lax.broadcasted_iota(jnp.int32, (2 * CAP, ROWS), 1)
    for s in range(CAP):
        mark = jnp.where((row == s) & (lane == chosen[0, 0, s]) & (s < count), 1.0, mark)
    owner[...] = mark.astype(BF)
    for copy in copies:
        copy.wait()
    x = dot(take_x.astype(BF), x_rows[...], 1, 0)
    y = dot(take_y.astype(BF), y_rows[...], 1, 0) * scale
    both = (x + y).astype(BF)
    place = place.astype(BF)
    for k in range(N_FSDP):
        part = both[:, k * DL : (k + 1) * DL]
        for i in range(N_DP):
            out[i * N_FSDP + k, :, 0:DL] = part
            out[i * N_FSDP + k, :, DL:MSG] = place


def messages(*operands):
    return pl.pallas_call(
        message_kernel,
        out_shape=[
            jax.ShapeDtypeStruct((N_DEV, 2 * CAP, MSG), BF),
            jax.ShapeDtypeStruct((2 * CAP, ROWS), BF),
        ],
        in_specs=[ANY] * 5,
        out_specs=[VMEM] * 2,
        scratch_shapes=[
            pltpu.SMEM((1, 1, CAP), jnp.int32),
            pltpu.SMEM((1, N_FSDP), jnp.int32),
            pltpu.SMEM((ROWS,), F32),
            pltpu.VMEM((CAP * 16, D), BF),
            pltpu.VMEM((CAP * 16, D), BF),
            pltpu.SemaphoreType.DMA((3,)),
            pltpu.SemaphoreType.DMA((2 * CAP,)),
        ],
        compiler_params=limits(60),
    )(*operands)


def pack_kernel(lines, out):
    places = jnp.transpose(lines[:, MSG - 128 : MSG].astype(F32)).astype(jnp.int32)
    spot = lax.broadcasted_iota(jnp.int32, (LIVE, N_DEV * 2 * CAP), 0)
    for k in range(2):
        at = DL - (MSG - 128) + k
        pack = jnp.where(places[at : at + 1, :] == spot, 1.0, 0.0).astype(BF)
        rows = dot(pack, lines[...], 1, 0).astype(BF)
        for i in range(N_DP):
            out[i, k * GROUP : (k + 1) * GROUP, :] = rows[i * GROUP : (i + 1) * GROUP]


def gather_rows(index, rows, order, x, y=None):
    for k, (dx, dz) in enumerate(order):
        i = (index[1] + dx) % 4 * 2 + (index[2] + dz) % 2
        here = slice(k * GROUP, (k + 1) * GROUP)
        x[here, :] = rows[i, 0:GROUP, :]
        if y is not None:
            y[here, :] = rows[i, GROUP : 2 * GROUP, :]


RELATIVE = tuple((dx, dz) for dx in range(4) for dz in range(2))


def products(index, own, sib, weights, lo, n, scratch, store):
    xo, yo, xs, ys, tail = scratch
    gather_rows(index, own, RELATIVE, xo, yo)
    gather_rows(index, sib, RELATIVE, xs, ys)
    for k in range(3):
        a, b = (xo, xs) if k < 2 else (yo, ys)
        ends = jnp.concatenate([a[:, 256:DL], b[:, 256:DL]], axis=1)
        mine, other = weights[2 * k], weights[2 * k + 1]
        tail[0 : DL - 256, 0:n] = mine[256:DL, lo : lo + n]
        tail[DL - 256 : 128, 0:n] = other[256:DL, lo : lo + n]
        for at in range(0, n, 256):
            to = min(at + 256, n)
            total = dot(a[:, 0:256], mine[0:256, lo + at : lo + to], 1, 0)
            total += dot(b[:, 0:256], other[0:256, lo + at : lo + to], 1, 0)
            total += dot(ends, tail[:, at:to], 1, 0)
            store(slice(k * n + at, k * n + to), total)


def kernel_b(index, own, sib, w0, w1, w2, w3, w4, w5, far0, far, near, *scratch):
    def store(cols, total):
        for dx in range(4):
            here, near_at = slice(dx * GROUP, (dx + 1) * GROUP), 2 * dx * GROUP
            near[here, cols] = total[near_at : near_at + GROUP]
            away = total[near_at + GROUP : near_at + 2 * GROUP].astype(BF)
            if dx:
                far[(dx - 1) * GROUP : dx * GROUP, cols] = away
            else:
                far0[:, cols] = away

    products(index, own, sib, (w0, w1, w2, w3, w4, w5), NA, NB, scratch, store)


def kernel_a(index, own, sib, w0, w1, w2, w3, w4, w5, here, right, two, left, *scratch):
    def store(cols, total):
        here[:, cols] = total[0 : 2 * GROUP]
        for k, out in enumerate((right, two, left)):
            out[:, cols] = total[(k + 1) * 2 * GROUP : (k + 2) * 2 * GROUP].astype(BF)

    products(index, own, sib, (w0, w1, w2, w3, w4, w5), 0, NA, scratch, store)


def local_products(kernel, n, shapes, *operands):
    rows = pltpu.VMEM((LIVE, MSG), BF)
    return call(
        kernel,
        [((r, 3 * n), kind) for r, kind in shapes],
        operands,
        scratch=[rows] * 4 + [pltpu.VMEM((128, n), BF)],
        smem=1,
        estimate=cost(2 * LIVE * 2 * DL * 3 * n, 10 * 2**20),
    )


def sum_b_kernel(near, far, right, two, left):
    for k, out in enumerate((right, two, left)):
        rows = slice((k + 1) * GROUP, (k + 2) * GROUP)
        out[...] = (near[rows] + far[k * GROUP : (k + 1) * GROUP].astype(F32)).astype(BF)


def sum_a_kernel(mine, a, b, c, here, far):
    def total(rows):
        return mine[rows] + a[rows].astype(F32) + b[rows].astype(F32) + c[rows].astype(F32)

    here[...] = total(slice(0, GROUP))
    far[...] = total(slice(GROUP, 2 * GROUP)).astype(BF)


def swiglu_backward(gate_pre, up_pre, hidden_delta):
    sigma = jax.nn.sigmoid(gate_pre)
    active = gate_pre * sigma
    hidden = active * up_pre
    gate_delta = hidden_delta * up_pre * sigma * (1.0 + gate_pre * (1.0 - sigma))
    up_delta = hidden_delta * active
    return hidden, gate_delta, up_delta


def value_kernel(index, mine_a, far_a, near, far0, right, two, left, out, piece, rest):
    sums_a = mine_a[...] + far_a[...].astype(F32)
    sums_b = near[0:GROUP] + far0[...].astype(F32) + right[...].astype(F32) + two[...].astype(F32) + left[...].astype(F32)
    of_a = swiglu_backward(*[sums_a[:, k * NA : (k + 1) * NA] for k in range(3)])
    of_b = swiglu_backward(*[sums_b[:, k * NB : (k + 1) * NB] for k in range(3)])
    unit = lax.broadcasted_iota(jnp.int32, (GROUP, NA), 1)
    keep = (unit >= TILE) | (index[3] == 0)
    for k in range(3):
        out[:, k * WIN : k * WIN + NA] = jnp.where(keep, of_a[k], 0.0).astype(BF)
        out[:, k * WIN + NA : (k + 1) * WIN] = of_b[k].astype(BF)
    piece[...] = out[:, :PART]
    rest[...] = out[:, PART:]


def lay_kernel(*refs):
    row = col = 0
    for block in refs[:-1]:
        width = block.shape[1]
        refs[-1][row * GROUP : (row + 1) * GROUP, col : col + width] = block[...]
        row, col = (row + 1, 0) if col + width == 3 * WIN else (row, width)


def laid(blocks):
    rows = sum(block.shape[1] for block in blocks) // (3 * WIN) * GROUP
    return call(lay_kernel, [((rows, 3 * WIN), BF)], blocks, estimate=cost(0, 4 * 2**20))[0]


def back_kernel(*refs):
    value, (go, gs, uo, us, mine, other) = refs[0], refs[1:]
    gate, up_w = value[:, WIN : 2 * WIN], value[:, 2 * WIN :]
    other[...] = dot(gate, gs[...], 1, 1) + dot(up_w, us[...], 1, 1)
    mine[...] = dot(gate, go[...], 1, 1) + dot(up_w, uo[...], 1, 1)


def back_products(value, weights):
    rows = value.shape[0]
    return call(
        back_kernel,
        [((rows, DL), F32)] * 2,
        [value, *weights],
        estimate=cost(2 * rows * DL * 4 * WIN, 6 * 2**20),
    )


def line_kernel(index, own, out):
    parts = []
    lane = DL + 2 - (MSG - 128)
    for dx, dz in ORDER:
        i = (index[1] + dx) % 4 * 2 + (index[2] + dz) % 2
        slot = own[i, 0:GROUP, MSG - 128 : MSG].astype(F32)[:, lane : lane + 1].astype(jnp.int32) - 1
        device = slot // CAP
        line = i * (N_FSDP // 2 * 2 * CAP) + device // 2 * (2 * CAP) + slot % CAP
        core = jnp.where(slot < 0, -1, device % 2)
        parts.append(jnp.concatenate([jnp.where(core == k, line, -2 * CAP) for k in range(2)], axis=1))
    lines = jnp.concatenate(parts, axis=0).astype(F32)
    lines = jnp.concatenate([lines, jnp.zeros((LIVE, 126), F32)], axis=1)
    out[...] = jnp.transpose(lines)[0:8, :].astype(jnp.int32)


def unpack(index, core, lines, parts, start=0):
    c = index[3]
    line = jnp.where(core == 0, lines[0:1, :], lines[1:2, :])
    mine = jnp.concatenate([part[...] for part in parts[0::2]])
    other = jnp.concatenate([part[...] for part in parts[1::2]])
    rows = mine.shape[0]
    line = line[:, start : start + rows]
    at = lax.broadcasted_iota(jnp.int32, (CAP * N_DEV, rows), 0)
    low = jnp.where(at == jnp.where(c == 0, line, line + CAP), 1.0, 0.0).astype(BF)
    high = jnp.where(at == jnp.where(c == 0, line + CAP, line), 1.0, 0.0).astype(BF)
    return dot(low, mine.astype(BF), 1, 0) + dot(high, other.astype(BF), 1, 0)


def unpack_early_kernel(index, lines, *refs):
    refs[-1][...] = unpack(index, 1 - index[3], lines, refs[:-1])


def unpack_last_kernel(index, lines, sent, value, go, gs, uo, us, mine, other, out):
    back_kernel(value, go, gs, uo, us, mine, other)
    last = unpack(index, 1 - index[3], lines, (mine, other), LIVE - GROUP)
    out[...] = (sent[...] + last).astype(BF)


def unpack_keep_kernel(index, lines, *refs):
    refs[-1][...] = unpack(index, index[3], lines, refs[:-1])


def add_kernel(kept, sent, out):
    out[...] = (kept[...] + sent[...].astype(F32)).astype(BF)


def owner_kernel(owner, back, out):
    n = N_FSDP // 2
    for k in range(n):
        total = back[k].astype(F32)
        for i in range(1, N_DP):
            total = total + back[i * n + k].astype(F32)
        total = total.astype(BF)
        for core in range(2):
            cols = slice((2 * k + core) * DL, (2 * k + core + 1) * DL)
            rows = slice(core * CAP, (core + 1) * CAP)
            out[:, cols] = dot(owner[0:CAP, :], total[rows, :], 0, 0).astype(BF)


def grad_kernel(index, own, early_in, late_in, early_other_in, late_other_in, gate_out, up_out,
                down_out, mine, other, x, y, gate, up_s, down_s, reads, sems):
    top, bottom = pl.ds(0, 4 * GROUP), pl.ds(4 * GROUP, 4 * GROUP)
    loads = [
        pltpu.make_async_copy(early_in, mine.at[top], reads.at[0]),
        pltpu.make_async_copy(late_in, mine.at[bottom], reads.at[1]),
        pltpu.make_async_copy(early_other_in, other.at[top], reads.at[2]),
        pltpu.make_async_copy(late_other_in, other.at[bottom], reads.at[3]),
    ]
    for copy in loads:
        copy.start()
    c = index[3]
    gather_rows(index, own, ORDER, x, y)
    starts = [pl.multiple_of(c * HI, 128), pl.multiple_of((1 - c) * HI, 128)]
    spans = [(lo, min(lo + 512, WIN)) for lo in range(0, WIN, 512)]
    copies = []
    for k, (scratch, result) in enumerate(((gate, gate_out), (up_s, up_out), (down_s, down_out))):
        part = (k + 1) % 3
        rows = (x if k < 2 else y)[:, 0:DL]

        def product(ref, lo, hi):
            return dot(rows, ref[:, part * WIN + lo : part * WIN + hi], 0, 0).astype(BF)

        for start, ref, first in zip(starts, (mine, other), (0, 2)):
            if k == 0:
                loads[first].wait()
                loads[first + 1].wait()
            for lo, hi in spans:
                scratch[:, pl.ds(start + lo, hi - lo)] = product(ref, lo, hi)

        @pl.when(c == 0)
        def _():
            scratch[:, HI:WIN] = product(mine, HI, WIN)

        @pl.when(c == 1)
        def _():
            scratch[:, HI:WIN] = product(other, HI, WIN)

        copies.append(pltpu.make_async_copy(scratch, result, sems.at[k]))
        copies[-1].start()
    for copy in copies:
        copy.wait()


def weight_grads(*operands):
    rows, grad = pltpu.VMEM((LIVE, MSG), BF), pltpu.VMEM((DL, FL), BF)
    values = pltpu.VMEM((LIVE, 3 * WIN), BF)
    return pl.pallas_call(
        grad_kernel,
        out_shape=[jax.ShapeDtypeStruct((DL, FL), BF)] * 3,
        in_specs=[SMEM, VMEM] + [ANY] * 4,
        out_specs=[ANY] * 3,
        scratch_shapes=[
            values, values, rows, rows, grad, grad, grad,
            pltpu.SemaphoreType.DMA((4,)),
            pltpu.SemaphoreType.DMA((3,)),
        ],
        compiler_params=limits(60),
        cost_estimate=cost(2 * LIVE * DL * FL * 3, 12 * 2**20),
    )(*operands)


def shards(tokens, cotangent, advantage, chosen, chosen_count, gate_weight, up_weight, down_weight):
    place = [lax.axis_index(a) for a in ("c", "x", "zl", "c")]
    index = jnp.stack(place).astype(jnp.int32)
    message, owner = messages(chosen, chosen_count, advantage, tokens, cotangent)
    message, gate_weight, up_weight, down_weight = lax.optimization_barrier(
        (message, gate_weight, up_weight, down_weight)
    )
    first = lax.axis_index("c") == 0

    def half(w, which):
        return jnp.where(which, w[:, :WIN], w[:, HI:])

    full = [gate_weight, up_weight, down_weight.T]
    halves = []
    for w in full:
        if halves:
            w, halves[-1] = lax.optimization_barrier((w, halves[-1]))
        halves.append(half(w, ~first))
    got = lax.all_to_all(message, AXES, 0, 0, tiled=True)
    got = lax.optimization_barrier((got, *halves))[0]
    own = call(pack_kernel, [((N_DP, 2 * GROUP, MSG), BF)], [got.reshape(N_DEV * 2 * CAP, MSG)])[0]
    own, *full = lax.optimization_barrier((own, *full))
    weights = [w for f, h in zip(full, halves) for w in (half(f, first), sibling(h))]
    sib = sibling(own)

    far0, far, near = local_products(
        kernel_b, NB, [(GROUP, BF), (3 * GROUP, BF), (4 * GROUP, F32)], index, own, sib, *weights
    )
    own_a, near = lax.optimization_barrier((own, near))
    here_a, right, two, left = local_products(
        kernel_a, NA, [(2 * GROUP, F32)] + [(2 * GROUP, BF)] * 3, index, own_a, sib, *weights
    )
    far0, far = across(far0), across(far)
    right, left, two = up(right), down(left), along(two, 2)
    shape_a, shape_b = (GROUP, 3 * NA), (GROUP, 3 * NB)
    right_b, two_b, left_b = call(sum_b_kernel, [(shape_b, BF)] * 3, [near, far])
    here_a, far_a = call(sum_a_kernel, [(shape_a, F32), (shape_a, BF)], [here_a, right, two, left])
    far_a = across(far_a)
    two_b, right_b, left_b = along(two_b, 2), up(right_b), down(left_b)
    v00, *p00 = call(
        value_kernel,
        [((GROUP, 3 * WIN), BF), ((GROUP, PART), BF), ((GROUP, 3 * WIN - PART), BF)],
        [index, here_a, far_a, near, far0, right_b, two_b, left_b],
        smem=1,
    )

    v10 = [down(p) for p in p00]
    v01, v30 = across(v00), up(v00)
    v10[0], v30 = lax.optimization_barrier((v10[0], v30))
    v10[1], v01 = lax.optimization_barrier((v10[1], v01))
    v20 = [down(p) for p in v10]
    v11 = [across(p) for p in v10]
    v31 = up(v01)
    early = laid([v00, v01, *v10, v30])
    backs = back_products(early, weights[:4])
    lines = call(line_kernel, [((8, LIVE), jnp.int32)], [index, own], smem=1)[0]
    v20[1], v31, early, lines = lax.optimization_barrier((v20[1], v31, early, lines))
    v21 = [across(p) for p in v20]
    backs += back_products(laid([*v20, *v11, v31]), weights[:4])
    shape, price = (CAP * N_DEV, DL), cost(2 * CAP * N_DEV * LIVE * DL, 2**20)
    sent = call(unpack_early_kernel, [(shape, F32)], [index, lines, *backs], smem=1, estimate=price)[0]
    v21[0], v21[1], sent, *backs = lax.optimization_barrier((*v21, sent, *backs))
    last = laid(v21)
    mine, other, sent = call(
        unpack_last_kernel,
        [((GROUP, DL), F32)] * 2 + [(shape, BF)],
        [index, lines, sent, last, *weights[:4]],
        smem=1,
        estimate=price,
    )
    backs += [mine, other]
    early_other = sibling(early)

    backs = [index, lines, *backs]
    last, sent = lax.optimization_barrier((last, sent))
    late = laid([*v20, *v11, v31, last])
    kept = call(unpack_keep_kernel, [(shape, F32)], backs, smem=1, estimate=price)[0]
    sent, late, kept = lax.optimization_barrier((sibling(sent), late, kept))
    late_other = sibling(late)
    back = call(add_kernel, [(shape, BF)], [kept, sent])[0]
    back = lax.all_to_all(back.reshape(N_DEV // 2, 2 * CAP, DL), AXES[:4], 0, 0, tiled=True)

    gate_grad, up_grad, down_grad = weight_grads(index, own, early, late, early_other, late_other)

    back, down_grad = lax.optimization_barrier((back, down_grad))
    input_grad = call(owner_kernel, [((ROWS, D), BF)], [owner, back])[0]
    return (input_grad, gate_grad, up_grad, down_grad.T)


def solution(mesh):
    fine = Mesh(mesh.devices.reshape(SIZES), AXES)
    dp, fsdp = AXES[:2], AXES[2:]
    in_specs = (
        P(AXES, None),
        P(AXES, None),
        P(AXES),
        P(dp, fsdp, None),
        P(dp, None),
        P(fsdp, dp),
        P(fsdp, dp),
        P(dp, fsdp),
    )
    out_specs = (P(AXES, None), P(fsdp, dp), P(fsdp, dp), P(dp, fsdp))
    return jax.shard_map(shards, mesh=fine, in_specs=in_specs, out_specs=out_specs, check_vma=False)
```
